32 devices in a mesh: groups: 2 (over y), chan: 4 (over z), seg: 2 (over x), freq: 2 (over core).
Axes of the slice: x: 2, y: 2, z: 4, core: 2. Of those that a mesh axis runs over, the one named last changes fastest.
Arguments:
- traces: bfloat16 [10, 1024, 4096], P('seg', ('groups', 'chan')), parts along dimension 1, may hold values from -120 to 120
- dead_mask: int32 [1024], P(('groups', 'chan')), parts along dimension 0, may hold values 0 or 1
- seg_counts: int32 [1024], P(('groups', 'chan')), parts along dimension 0, may hold values from 1 to 10
- offsets: int32 [4], replicated, may hold values from 1 to 128, as said below
Outputs:
- correlations: float32 [1024, 4, 512], P(('groups', 'chan', 'seg'), None, 'freq'), parts along dimension 0
The draws below stay inside these ranges and needn't reach their ends.
There are 2 independent parts, one for each index of `groups`. The reference program is written for one: setup_inputs(seed, part) draws one part's arguments, and reference() takes and returns one part's arrays. A program takes and returns all parts, laid end to end along the dimension named above; an argument that names none is the same for every part. Nothing has to cross between parts.
Inputs may be any that keep to these rules, and one draw needn't show every extreme that they name: The 4 offsets are distinct and one of them equals 128.
All inputs are finite; a program needn't handle non-finite values. No bound on the sum of `dead_mask` on one device may be relied on, other than what follows from the above.
Results may differ from the reference program's by a relative error of at most 0.0056.
Values may be sent and summed in bfloat16 or wider, within the bound.
No kernel may reach another device: no remote copies, remote signals or barrier semaphores. Data moves between devices by JAX's collectives and lax.ppermute only.
A program may use at most 128 MiB of HBM per device.

```python
import math
import jax
import jax.numpy as jnp
from jax import lax

L = 4096
HALF = 32
LAGS = 512
K = 4
F = 2048
BAND = 128
C = 512
SEGS = 10


def draw_traces(key, part):
    gain_key, tap_key, noise_key = jax.random.split(key, 3)
    gains = jnp.exp(jax.random.uniform(gain_key, (1, C, 1), jnp.float32, 0.0, 2.302585))
    taps = jax.random.uniform(tap_key, (3, 1, C, 1), jnp.float32, -1.0, 1.0)
    tap_one = 0.9 * taps[0]
    tap_two = 0.6 * taps[1]
    tap_three = 0.3 * taps[2]
    noise = jnp.clip(jax.random.normal(noise_key, (SEGS, C, L + 3), jnp.float32), -4.0, 4.0)
    filtered = noise[:, :, 3:] + tap_one * noise[:, :, 2:-1] + tap_two * noise[:, :, 1:-2] + tap_three * noise[:, :, :-3]
    return (gains * filtered).astype(jnp.bfloat16)


def draw_offsets(key, part):
    chosen = jax.random.permutation(jax.random.fold_in(key, 11), BAND - 1)[:K - 1] + 1
    values = jnp.concatenate([chosen.astype(jnp.int32), jnp.full((1,), BAND, jnp.int32)])
    order = jax.random.permutation(jax.random.fold_in(key, 12), K)
    return values[order].astype(jnp.int32)


def place_ends(entries, rng, low, high):
    dims = entries.shape
    spot = [jax.random.randint(jax.random.fold_in(rng, axis), (), 0, dims[axis]) for axis in range(len(dims))]
    entries = entries.at[tuple(spot)].set(low)
    longest = dims.index(max(dims))
    spot[longest] = (spot[longest] + 1) % dims[longest]
    return entries.at[tuple(spot)].set(high)


def setup_inputs(seed: int = 0, part: int = 0) -> dict:
    streams_of = jax.random.split(jax.random.key(seed), 5)
    part_splits = jax.random.split(jax.random.fold_in(streams_of[4], part), 5)
    traces = draw_traces(jax.random.fold_in(jax.random.fold_in(streams_of[4], part), 71), part)
    dead_mask = place_ends((jax.random.randint(part_splits[1], (C,), 0, 8) < 7).astype(jnp.int32), jax.random.fold_in(part_splits[1], 1), 0, 1)
    seg_counts = place_ends(jax.random.randint(part_splits[2], (C,), 1, SEGS + 1), jax.random.fold_in(part_splits[2], 1), 1, SEGS).astype(jnp.int32)
    offsets = draw_offsets(jax.random.fold_in(streams_of[4], 71), part)
    return {"traces": traces, "dead_mask": dead_mask, "seg_counts": seg_counts, "offsets": offsets}


epsilon = 1e-06

def fourier_table(bin_first, bin_number, length):
    samples = jnp.arange(length, dtype=jnp.int32)[:, None]
    bin_index = bin_first + jnp.arange(bin_number, dtype=jnp.int32)[None, :]
    phases = (samples * bin_index % length).astype(jnp.float32) * (2.0 * math.pi / length)
    return jnp.concatenate([jnp.cos(phases), -jnp.sin(phases)], axis=1).astype(jnp.bfloat16)

def delay_table(bin_first, bin_number, length, lag_number, bin_total):
    bin_index = bin_first + jnp.arange(bin_number, dtype=jnp.int32)[:, None]
    shifts = jnp.arange(lag_number, dtype=jnp.int32)[None, :] - lag_number // 2
    phases = (bin_index * shifts % length).astype(jnp.float32) * (2.0 * math.pi / length)
    scaling = 1.0 / math.sqrt(bin_total)
    return jnp.concatenate([jnp.cos(phases) * scaling, -jnp.sin(phases) * scaling], axis=0)

def reference(traces, dead_mask, seg_counts, offsets):
    fourier = fourier_table(0, F, L).astype(jnp.float32)
    bin_index = jnp.arange(F, dtype=jnp.int32)
    window_count = (jnp.minimum(bin_index + HALF, F - 1) - jnp.maximum(bin_index - HALF, 0) + 1).astype(jnp.float32)
    alive = dead_mask.astype(jnp.float32)
    zero_rows = jnp.zeros((BAND, F), jnp.float32)

    def segment(stacked, inputs):
        samples, seg_number = inputs
        spectra = jnp.dot(samples.astype(jnp.float32), fourier, precision=lax.Precision.HIGHEST)
        real_part = spectra[:, :F]
        imag_part = spectra[:, F:]
        power_bins = real_part * real_part + imag_part * imag_part
        window_sum = lax.reduce_window(power_bins, jnp.zeros((), power_bins.dtype), lax.add, (1, 2 * HALF + 1), (1, 1), ((0, 0), (HALF, HALF)))
        valid_seg = alive * (seg_number < seg_counts).astype(jnp.float32)
        factor = valid_seg[:, None] / jnp.sqrt(window_sum / window_count + epsilon)
        white_re = real_part * factor
        white_im = imag_part * factor
        padded_re = jnp.concatenate([white_re, zero_rows], axis=0)
        padded_im = jnp.concatenate([white_im, zero_rows], axis=0)
        slots = []
        for slot in range(K):
            partner_re = lax.dynamic_slice_in_dim(padded_re, offsets[slot], C, 0)
            partner_im = lax.dynamic_slice_in_dim(padded_im, offsets[slot], C, 0)
            slots.append(jnp.concatenate([white_re * partner_re + white_im * partner_im, white_im * partner_re - white_re * partner_im], axis=1))
        return (stacked + jnp.stack(slots, axis=1), None)
    initial = jnp.zeros((C, K, 2 * F), jnp.float32)
    seg_numbers = jnp.arange(SEGS, dtype=jnp.int32)
    stacked, unused = lax.scan(segment, initial, (traces, seg_numbers))
    padded_counts = jnp.concatenate([seg_counts, jnp.zeros((BAND,), jnp.int32)])
    divisors = []
    for slot in range(K):
        partner_count = lax.dynamic_slice_in_dim(padded_counts, offsets[slot], C, 0)
        divisors.append(jnp.maximum(jnp.minimum(seg_counts, partner_count), 1).astype(jnp.float32))
    divisor = jnp.stack(divisors, axis=1)
    cross = stacked / divisor[:, :, None]
    delay = delay_table(0, F, L, LAGS, F)
    return jnp.einsum('ckf,fl->ckl', cross, delay, precision=lax.Precision.HIGHEST)
```

```python
import math

import jax
import jax.numpy as jnp
import numpy as np
from jax import lax
from jax.experimental import pallas as pl
from jax.experimental.pallas import tpu as pltpu
from jax.sharding import PartitionSpec as P
import ml_dtypes

HALF = 32
LAGS = 512
F = 2048
TILE = 128
EPSILON = 1e-06
MIB = 1 << 20


def tables(length, parts):
    bins_dev = F // parts
    tiles = bins_dev // TILE
    cosines = np.cos(np.arange(length) * (2.0 * math.pi / length))
    sines = -np.sin(np.arange(length) * (2.0 * math.pi / length))
    cos16 = cosines.astype(np.float32).astype(ml_dtypes.bfloat16)
    sin16 = sines.astype(np.float32).astype(ml_dtypes.bfloat16)
    samples = np.arange(length)[:, None]
    fourier = np.zeros((parts, tiles + 1, length, 2 * TILE), ml_dtypes.bfloat16)
    for part in range(parts):
        for tile in range(tiles + 1):
            first = part * bins_dev + (tile - 1) * TILE
            bin_index = first + np.arange(TILE)
            keep = np.ones((TILE,), bool)
            if tile == 0:
                lane = np.arange(TILE)
                after = part * bins_dev + bins_dev + lane
                before = part * bins_dev - TILE + lane
                bin_index = np.where(lane < HALF, after, before)
                keep = ((lane < HALF) & (after < F)) | ((lane >= TILE - HALF) & (before >= 0))
            phases = samples * bin_index[None, :] % length
            zero = ml_dtypes.bfloat16(0)
            fourier[part, tile, :, :TILE] = np.where(keep, cos16[phases], zero)
            fourier[part, tile, :, TILE:] = np.where(keep, sin16[phases], zero)
    lag_part = LAGS // parts
    delay = np.zeros((parts, 2 * bins_dev, LAGS), ml_dtypes.bfloat16)
    scaling = 1.0 / math.sqrt(F)
    for part in range(parts):
        shifts = np.roll(np.arange(LAGS), -part * lag_part) - LAGS // 2
        for tile in range(tiles):
            bin_index = part * bins_dev + tile * TILE + np.arange(TILE)
            phases = bin_index[:, None] * shifts[None, :] % length
            rows = tile * 2 * TILE
            delay[part, rows : rows + TILE] = (cosines[phases] * scaling).astype(ml_dtypes.bfloat16)
            delay[part, rows + TILE : rows + 2 * TILE] = (sines[phases] * scaling).astype(ml_dtypes.bfloat16)
    band = np.abs(np.arange(3 * TILE)[:, None] - TILE - np.arange(TILE)[None, :]) <= HALF
    return fourier, delay, band.astype(ml_dtypes.bfloat16)


def whiten_kernel(tiles, part_ref, x_ref, table_ref, band_ref, valid_ref, lo_ref, hi_ref, spectra, power):
    step = pl.program_id(0)
    segs, half, _ = lo_ref.shape

    def transform():
        block = jnp.dot(x_ref[...], table_ref[...], preferred_element_type=jnp.float32)
        spectra[step] = block
        re, im = block[:, :TILE], block[:, TILE:]
        power[step] = (re * re + im * im).astype(jnp.bfloat16)

    def finish():
        tile = step - 2
        after = lax.rem(tile + 1, tiles + 1)
        window = jnp.dot(power[tile - 1], band_ref[:TILE], preferred_element_type=jnp.float32)
        window += jnp.dot(power[tile], band_ref[TILE : 2 * TILE], preferred_element_type=jnp.float32)
        window += jnp.dot(power[after], band_ref[2 * TILE :], preferred_element_type=jnp.float32)
        first = part_ref[0] * (tiles * TILE) + (tile - 1) * TILE
        bin_index = first + lax.broadcasted_iota(jnp.int32, (1, TILE), 1)
        count = jnp.minimum(bin_index + HALF, F - 1) - jnp.maximum(bin_index - HALF, 0) + 1
        inverse = 1.0 / count.astype(jnp.float32)
        factor = valid_ref[...] * lax.rsqrt(window * inverse + EPSILON)
        re = (spectra[tile, :, :TILE] * factor).astype(jnp.bfloat16)
        im = (spectra[tile, :, TILE:] * factor).astype(jnp.bfloat16)
        for seg in range(segs):
            row = seg * 2 * half
            lo_ref[seg, :, :TILE] = re[row : row + half]
            lo_ref[seg, :, TILE:] = im[row : row + half]
            hi_ref[seg, :, :TILE] = re[row + half : row + 2 * half]
            hi_ref[seg, :, TILE:] = im[row + half : row + 2 * half]

    @pl.when(step < 3)
    def _():
        transform()

    @pl.when((step >= 3) & (step <= tiles))
    def _():
        transform()
        finish()

    @pl.when(step > tiles)
    def _():
        finish()


def whiten(part, traces, fourier, band, valid):
    segs, chans, length = traces.shape
    rows, half = segs * chans, chans // 2
    tiles = fourier.shape[1] - 1
    out = jax.ShapeDtypeStruct((segs, half, 2 * TILE * tiles), jnp.bfloat16)
    out_spec = pl.BlockSpec((segs, half, 2 * TILE), lambda j, p: (0, 0, jnp.clip(j - 3, 0, tiles - 1)))
    return pl.pallas_call(
        lambda *refs: whiten_kernel(tiles, *refs),
        out_shape=(out, out),
        grid_spec=pltpu.PrefetchScalarGridSpec(
            num_scalar_prefetch=1,
            grid=(tiles + 3,),
            in_specs=[
                pl.BlockSpec((rows, length), lambda j, p: (0, 0)),
                pl.BlockSpec((None, None, length, 2 * TILE), lambda j, p: (p[0], jnp.minimum(j, tiles), 0, 0)),
                pl.BlockSpec((3 * TILE, TILE), lambda j, p: (0, 0)),
                pl.BlockSpec((rows, TILE), lambda j, p: (0, 0)),
            ],
            out_specs=[out_spec, out_spec],
            scratch_shapes=[
                pltpu.VMEM((tiles + 1, rows, 2 * TILE), jnp.float32),
                pltpu.VMEM((tiles + 1, rows, TILE), jnp.bfloat16),
            ],
        ),
        compiler_params=pltpu.CompilerParams(vmem_limit_bytes=40 * MIB),
        cost_estimate=pl.CostEstimate(
            flops=2 * rows * length * 2 * TILE * (tiles + 1),
            bytes_accessed=2 * length * 2 * TILE * (tiles + 1),
            transcendentals=0,
        ),
        name="whiten",
    )(part, traces.reshape(rows, length), fourier, band, valid)


def correlate_kernel(
    scalars, before_ref, lo_ref, hi_ref, after_ref, delay_ref, keep_ref, send_ref, frame, cross, total
):
    step, last = pl.program_id(0), pl.num_programs(0) - 1
    segs, half, _ = lo_ref.shape
    chans = 2 * half
    slots = cross.shape[0]
    keep = keep_ref.shape[2]
    for seg in range(segs):
        for place, ref in enumerate((before_ref, lo_ref, hi_ref, after_ref)):
            block = ref[seg].astype(jnp.float32)
            frame[seg, 0, place * half : (place + 1) * half] = block[:, :TILE]
            frame[seg, 1, place * half : (place + 1) * half] = block[:, TILE:]

    for slot in range(slots):
        offset = scalars[1 + slot]
        own_first = jnp.minimum(half, chans - offset)

        def rows(index, carry, slot=slot, own_first=own_first, offset=offset):
            real = jnp.zeros((16, TILE), jnp.float32)
            imag = jnp.zeros((16, TILE), jnp.float32)
            base = own_first + index * 16
            for seg in range(segs):
                own_re = frame[seg, 0, pl.ds(base, 16), :]
                own_im = frame[seg, 1, pl.ds(base, 16), :]
                far_re = frame[seg, 0, pl.ds(base + offset, 16), :]
                far_im = frame[seg, 1, pl.ds(base + offset, 16), :]
                real += own_re * far_re + own_im * far_im
                imag += own_im * far_re - own_re * far_im
            spot = pl.ds(pl.multiple_of(index * 16, 16), 16)
            cross[slot, spot, :TILE] = real.astype(jnp.bfloat16)
            cross[slot, spot, TILE:] = imag.astype(jnp.bfloat16)
            return carry

        lax.fori_loop(0, chans // 16, rows, 0)
        part = jnp.dot(cross[slot], delay_ref[...], preferred_element_type=jnp.float32)

        @pl.when(step == 0)
        def _(slot=slot, part=part):
            total[slot] = part

        @pl.when(step > 0)
        def _(slot=slot, part=part):
            total[slot] += part

    @pl.when(step == last)
    def _():
        keep_ref[...] = jnp.zeros_like(keep_ref)
        for slot in range(slots):
            offset = scalars[1 + slot]
            own_first = jnp.minimum(half, chans - offset)
            frame[0, 0, : chans + half] = jnp.zeros((chans + half, TILE), jnp.float32)
            for lane in range(total.shape[2] // TILE):
                frame[0, 0, pl.ds(own_first, chans), :] = total[slot, :, lane * TILE : (lane + 1) * TILE]
                placed = frame[0, 0, : chans + half]
                at = lane * TILE
                if at < keep:
                    keep_ref[slot, :, at : at + TILE] = placed
                else:
                    send_ref[slot, :, at - keep : at - keep + TILE] = placed.astype(send_ref.dtype)


def correlate(scalars, before, lo, hi, after, delay, parts):
    segs, half, columns = lo.shape
    tiles = columns // (2 * TILE)
    slots = scalars.shape[0] - 1
    lags = delay.shape[2]
    rows = 3 * half
    spec = pl.BlockSpec((segs, half, 2 * TILE), lambda j, s: (0, 0, j))
    whole = lambda width: pl.BlockSpec((slots, rows, width), lambda j, s: (0, 0, 0))
    keep = lags // parts
    return pl.pallas_call(
        correlate_kernel,
        out_shape=(
            jax.ShapeDtypeStruct((slots, rows, keep), jnp.float32),
            jax.ShapeDtypeStruct((slots, rows, lags - keep), jnp.bfloat16),
        ),
        grid_spec=pltpu.PrefetchScalarGridSpec(
            num_scalar_prefetch=1,
            grid=(tiles,),
            in_specs=[spec, spec, spec, spec, pl.BlockSpec((None, 2 * TILE, lags), lambda j, s: (s[0], j, 0))],
            out_specs=[whole(keep), whole(lags - keep)],
            scratch_shapes=[
                pltpu.VMEM((segs, 2, 4 * half, TILE), jnp.float32),
                pltpu.VMEM((slots, 2 * half, 2 * TILE), jnp.bfloat16),
                pltpu.VMEM((slots, 2 * half, lags), jnp.float32),
            ],
        ),
        compiler_params=pltpu.CompilerParams(vmem_limit_bytes=40 * MIB),
        name="correlate",
    )(scalars, before, lo, hi, after, delay)


def shift(block, axis, distance):
    devices = range(lax.axis_size(axis))
    return lax.ppermute(block, axis, [(i, i + distance) for i in devices if i + distance in devices])


def shards(traces, dead_mask, seg_counts, offsets):
    segs, chans, length = traces.shape
    half = chans // 2
    parts = lax.axis_size("freq")
    spans = lax.axis_size("seg")
    assert parts == 2
    fourier, delay, band = tables(length, parts)
    part = lax.axis_index("freq")
    span = lax.axis_index("seg")
    seg_index = span * segs + jnp.arange(segs, dtype=jnp.int32)
    valid = (seg_index[:, None] < seg_counts[None, :]) & (dead_mask[None, :] > 0)
    valid = jnp.broadcast_to(valid.astype(jnp.float32).reshape(segs * chans, 1), (segs * chans, TILE))
    next_counts = shift(seg_counts, "chan", -1)
    lo, hi = whiten(part.reshape(1).astype(jnp.int32), traces, jnp.asarray(fourier), jnp.asarray(band), valid)
    before = shift(hi, "chan", 1)
    after = shift(lo, "chan", -1)
    scalars = jnp.concatenate([part.reshape(1).astype(jnp.int32), offsets])
    keep, send = correlate(scalars, before, lo, hi, after, jnp.asarray(delay), parts)
    keep = keep + lax.ppermute(send, "freq", [(0, 1), (1, 0)]).astype(jnp.float32)
    back = shift(keep[:, :half].astype(jnp.bfloat16), "chan", -1).astype(jnp.float32)
    keep = keep[:, half:]
    keep = keep + jnp.pad(back, ((0, 0), (chans - half, 0), (0, 0)))
    piece = chans // spans
    result = lax.dynamic_slice_in_dim(keep, span * piece, piece, 1)
    for step in range(1, spans):
        target = lax.rem(span + step, spans)
        block = lax.dynamic_slice_in_dim(keep, target * piece, piece, 1).astype(jnp.bfloat16)
        result = result + lax.ppermute(block, "seg", [(i, (i + step) % spans) for i in range(spans)]).astype(jnp.float32)
    all_counts = jnp.concatenate([seg_counts, next_counts])
    inverses = []
    for slot in range(offsets.shape[0]):
        own = lax.dynamic_slice_in_dim(all_counts, span * piece, piece, 0)
        far = lax.dynamic_slice_in_dim(all_counts, span * piece + offsets[slot], piece, 0)
        inverses.append(1.0 / jnp.maximum(jnp.minimum(own, far), 1).astype(jnp.float32))
    inverse = jnp.stack(inverses, axis=0)
    return jnp.transpose(result * inverse[:, :, None], (1, 0, 2))


def solution(mesh):
    in_specs = (
        P("seg", ("groups", "chan"), None),
        P(("groups", "chan")),
        P(("groups", "chan")),
        P(),
    )
    out_specs = P(("groups", "chan", "seg"), None, "freq")
    return jax.shard_map(shards, mesh=mesh, in_specs=in_specs, out_specs=out_specs, check_vma=False)
```

```python
import functools
import math

import jax
import jax.numpy as jnp
import numpy as np
from jax import lax
from jax.experimental import pallas as pl
from jax.experimental.pallas import tpu as pltpu
from jax.sharding import PartitionSpec as P
import ml_dtypes

HALF = 32
LAGS = 512
F = 2048
TILE = 128
EPSILON = 1e-06
MIB = 1 << 20
CHUNKS = 8
GROUPS = (5, 9)


def tables(length, parts):
    bins_dev = F // parts
    tiles = bins_dev // TILE
    cosines = np.cos(np.arange(length) * (2.0 * math.pi / length))
    sines = -np.sin(np.arange(length) * (2.0 * math.pi / length))
    cos16 = cosines.astype(np.float32).astype(ml_dtypes.bfloat16)
    sin16 = sines.astype(np.float32).astype(ml_dtypes.bfloat16)
    samples = np.arange(length)[:, None]
    fourier = np.zeros((parts, tiles + 1, length, 2 * TILE), ml_dtypes.bfloat16)
    for part in range(parts):
        for tile in range(tiles + 1):
            first = part * bins_dev + (tile - 1) * TILE
            bin_index = first + np.arange(TILE)
            keep = np.ones((TILE,), bool)
            if tile == 0:
                lane = np.arange(TILE)
                after = part * bins_dev + bins_dev + lane
                before = part * bins_dev - TILE + lane
                bin_index = np.where(lane < HALF, after, before)
                keep = ((lane < HALF) & (after < F)) | ((lane >= TILE - HALF) & (before >= 0))
            phases = samples * bin_index[None, :] % length
            zero = ml_dtypes.bfloat16(0)
            fourier[part, tile, :, :TILE] = np.where(keep, cos16[phases], zero)
            fourier[part, tile, :, TILE:] = np.where(keep, sin16[phases], zero)
    lag_part = LAGS // parts
    delay = np.zeros((parts, 2 * bins_dev, LAGS), ml_dtypes.bfloat16)
    scaling = 1.0 / math.sqrt(F)
    for part in range(parts):
        shifts = np.roll(np.arange(LAGS), -part * lag_part) - LAGS // 2
        for tile in range(tiles):
            bin_index = part * bins_dev + tile * TILE + np.arange(TILE)
            phases = bin_index[:, None] * shifts[None, :] % length
            rows = tile * 2 * TILE
            delay[part, rows : rows + TILE] = (cosines[phases] * scaling).astype(ml_dtypes.bfloat16)
            delay[part, rows + TILE : rows + 2 * TILE] = (sines[phases] * scaling).astype(ml_dtypes.bfloat16)
    band = np.abs(np.arange(3 * TILE)[:, None] - TILE - np.arange(TILE)[None, :]) <= HALF
    return fourier, delay, band.astype(ml_dtypes.bfloat16)


def whiten_kernel(plan, scalars, x_hbm, table_ref, band_ref, counts_ref, alive_ref, *refs):
    (first, stop), _, tiles = plan
    refs = list(refs)
    carried = (refs.pop(0), refs.pop(0)) if first else None
    lo_ref, hi_ref = refs.pop(0), refs.pop(0)
    handed = (refs.pop(0), refs.pop(0)) if stop <= tiles else None
    x, sems, eff, spectra, power = refs
    step = pl.program_id(0)
    made = stop - first
    segs, half, _ = lo_ref.shape
    chans = 2 * half
    chunk = x.shape[1] // CHUNKS
    edge = 0 if first else 3
    lag = 1 if first else 3

    def fetch(index):
        part = pl.ds(index * chunk, chunk)
        return pltpu.make_async_copy(x_hbm.at[:, part], x.at[:, part], sems.at[index])

    def store(block):
        slot = step + 1
        spectra[slot] = block
        re, im = block[:, :TILE], block[:, TILE:]
        power[slot + 2] = (re * re + im * im).astype(jnp.bfloat16)

    def finish():
        tile = first + step - 2
        slot = step - 1
        before, after = slot + 1, jnp.where(tile == tiles, edge, slot + 3)
        window = jnp.dot(power[before], band_ref[:TILE], preferred_element_type=jnp.float32)
        window += jnp.dot(power[slot + 2], band_ref[TILE : 2 * TILE], preferred_element_type=jnp.float32)
        window += jnp.dot(power[after], band_ref[2 * TILE :], preferred_element_type=jnp.float32)
        bin_index = scalars[0] * (tiles * TILE) + (tile - 1) * TILE + lax.broadcasted_iota(jnp.int32, (1, TILE), 1)
        count = jnp.minimum(bin_index + HALF, F - 1) - jnp.maximum(bin_index - HALF, 0) + 1
        inverse = 1.0 / count.astype(jnp.float32)
        for seg in range(segs):
            row = seg * chans
            scale = lax.rsqrt(window[row : row + chans] * inverse + EPSILON)
            number = (scalars[1] + seg).astype(jnp.float32)
            scale = jnp.where(number < eff[...], scale, 0.0)
            re = (spectra[slot, row : row + chans, :TILE] * scale).astype(jnp.bfloat16)
            im = (spectra[slot, row : row + chans, TILE:] * scale).astype(jnp.bfloat16)
            lo_ref[seg, :, :TILE] = re[:half]
            lo_ref[seg, :, TILE:] = im[:half]
            hi_ref[seg, :, :TILE] = re[half:]
            hi_ref[seg, :, TILE:] = im[half:]

    @pl.when(step == 0)
    def _():
        for index in range(CHUNKS):
            fetch(index).start()
        row = jnp.where(alive_ref[...] > 0, counts_ref[...], 0).astype(jnp.float32)
        eff[...] = jnp.transpose(jnp.broadcast_to(row, (chans, chans)))
        if carried:
            spectra[0] = carried[0][...]
            power[0:3] = carried[1][...]
        block = None
        for index in range(CHUNKS):
            fetch(index).wait()
            part = slice(index * chunk, (index + 1) * chunk)
            term = jnp.dot(x[:, part], table_ref[part], preferred_element_type=jnp.float32)
            block = term if block is None else block + term
        store(block)

    if lag > 1:

        @pl.when((step >= 1) & (step < lag))
        def _():
            store(jnp.dot(x[...], table_ref[...], preferred_element_type=jnp.float32))

    @pl.when((step >= lag) & (step < made))
    def _():
        finish()
        store(jnp.dot(x[...], table_ref[...], preferred_element_type=jnp.float32))

    @pl.when(step >= made)
    def _():
        finish()

    if handed:

        @pl.when(step == made)
        def _():
            handed[0][...] = spectra[made]
            handed[1][0] = power[edge]
            handed[1][1] = power[made + 1]
            handed[1][2] = power[made + 2]


def whiten(plan, scalars, rows, fourier, band, counts, alive, carried, segs):
    (first, stop), (done_first, done_stop), tiles = plan
    made, done = stop - first, done_stop - done_first
    total, length = rows.shape
    half = total // segs // 2
    lag = 1 if first else 3
    steps = done + lag
    out = jax.ShapeDtypeStruct((segs, half, 2 * TILE * done), jnp.bfloat16)
    out_spec = pl.BlockSpec((segs, half, 2 * TILE), lambda j, p: (0, 0, jnp.clip(j - lag, 0, done - 1)))
    out_shape, out_specs = [out, out], [out_spec, out_spec]
    carry_spec = [
        pl.BlockSpec((total, 2 * TILE), lambda j, p: (0, 0)),
        pl.BlockSpec((3, total, TILE), lambda j, p: (0, 0, 0)),
    ]
    if stop <= tiles:
        out_shape += [
            jax.ShapeDtypeStruct((total, 2 * TILE), jnp.float32),
            jax.ShapeDtypeStruct((3, total, TILE), jnp.bfloat16),
        ]
        out_specs += carry_spec
    vector = pl.BlockSpec((1, 2 * half), lambda j, p: (0, 0))
    return pl.pallas_call(
        functools.partial(whiten_kernel, plan),
        out_shape=out_shape,
        grid_spec=pltpu.PrefetchScalarGridSpec(
            num_scalar_prefetch=1,
            grid=(steps,),
            in_specs=[
                pl.BlockSpec(memory_space=pl.ANY),
                pl.BlockSpec(
                    (None, None, length, 2 * TILE), lambda j, p: (p[0], jnp.minimum(first + j, stop - 1), 0, 0)
                ),
                pl.BlockSpec((3 * TILE, TILE), lambda j, p: (0, 0)),
                vector,
                vector,
            ]
            + (carry_spec if first else []),
            out_specs=out_specs,
            scratch_shapes=[
                pltpu.VMEM((total, length), jnp.bfloat16),
                pltpu.SemaphoreType.DMA((CHUNKS,)),
                pltpu.VMEM((2 * half, 2 * half), jnp.float32),
                pltpu.VMEM((made + 1, total, 2 * TILE), jnp.float32),
                pltpu.VMEM((made + 3, total, TILE), jnp.bfloat16),
            ],
        ),
        compiler_params=pltpu.CompilerParams(vmem_limit_bytes=48 * MIB),
        cost_estimate=pl.CostEstimate(
            flops=2 * total * length * 2 * TILE * made,
            bytes_accessed=2 * length * 2 * TILE * made + 2 * total * length,
            transcendentals=0,
        ),
        name="whiten",
    )(scalars, rows, fourier, band, counts, alive, *carried)


def window_start(offset, chans):
    return jnp.minimum(chans // 2, chans - offset) // 16 * 16


def correlate_kernel(plan, scalars, before_ref, lo_ref, hi_ref, after_ref, delay_ref, *refs):
    tile_first, is_first, is_last = plan
    refs = list(refs)
    if is_first:
        own_counts, next_counts = refs.pop(0), refs.pop(0)
    else:
        sum_ref = refs.pop(0)
    if is_last:
        keep_ref, send_ref = refs.pop(0), refs.pop(0)
    else:
        total = refs.pop(0)
    if is_first:
        inverse_ref = refs.pop(0)
    if is_last:
        total = refs.pop(0)
    select, frame, far, cross = refs
    step, last = pl.program_id(0), pl.num_programs(0) - 1
    segs, half, _ = lo_ref.shape
    chans = 2 * half
    slots = cross.shape[0] // chans

    @pl.when(step == 0)
    def _():
        total[...] = jnp.zeros_like(total) if is_first else sum_ref[...]
        row = lax.broadcasted_iota(jnp.int32, (chans, 2 * chans), 0)
        column = lax.broadcasted_iota(jnp.int32, (chans, 2 * chans), 1)
        for slot in range(slots):
            offset = scalars[1 + slot]
            match = column == row + window_start(offset, chans) + offset
            select[slot * chans : (slot + 1) * chans] = match.astype(jnp.float32).astype(jnp.bfloat16)
        if is_first:
            row = lax.broadcasted_iota(jnp.int32, (chans, chans), 0)
            column = lax.broadcasted_iota(jnp.int32, (chans, chans), 1)
            own, following = own_counts[...].astype(jnp.float32), next_counts[...].astype(jnp.float32)
            mine = jnp.sum(jnp.where(row == column, own, 0.0), axis=1, keepdims=True)
            for slot in range(slots):
                target = row + scalars[1 + slot]
                partner = jnp.where(column == target, own, 0.0) + jnp.where(column + chans == target, following, 0.0)
                partner = jnp.sum(partner, axis=1, keepdims=True)
                divisor = jnp.maximum(jnp.minimum(mine, partner), 1.0)
                inverse_ref[slot] = jnp.broadcast_to(1.0 / divisor, (chans, TILE))

    for seg in range(segs):
        for place, ref in enumerate((before_ref, lo_ref, hi_ref, after_ref)):
            frame[seg, place * half : (place + 1) * half] = ref[seg]
    for seg in range(segs):
        far[seg] = jnp.dot(select[...], frame[seg], preferred_element_type=jnp.float32)
    for slot in range(slots):
        start = window_start(scalars[1 + slot], chans)

        def rows(index, carry, slot=slot, start=start):
            real = jnp.zeros((16, TILE), jnp.float32)
            imag = jnp.zeros((16, TILE), jnp.float32)
            base = pl.multiple_of(start + index * 16, 16)
            spot = pl.multiple_of(slot * chans + index * 16, 16)
            for seg in range(segs):
                own = frame[seg, pl.ds(base, 16), :].astype(jnp.float32)
                own_re, own_im = own[:, :TILE], own[:, TILE:]
                far_re, far_im = far[seg, pl.ds(spot, 16), :TILE], far[seg, pl.ds(spot, 16), TILE:]
                real += own_re * far_re + own_im * far_im
                imag += own_im * far_re - own_re * far_im
            cross[pl.ds(spot, 16), :TILE] = real.astype(jnp.bfloat16)
            cross[pl.ds(spot, 16), TILE:] = imag.astype(jnp.bfloat16)
            return carry

        lax.fori_loop(0, chans // 16, rows, 0, unroll=True)
    total[...] += jnp.dot(cross[...], delay_ref[...], preferred_element_type=jnp.float32)

    if is_last:

        @pl.when(step == last)
        def _():
            keep = keep_ref.shape[2]
            keep_ref[...] = jnp.zeros_like(keep_ref)
            send_ref[...] = jnp.zeros_like(send_ref)
            for slot in range(slots):
                start = pl.multiple_of(window_start(scalars[1 + slot], chans), 16)
                block = total[slot * chans : (slot + 1) * chans]
                keep_ref[slot, pl.ds(start, chans), :] = block[:, :keep]
                send_ref[slot, pl.ds(start, chans), :] = block[:, keep:].astype(send_ref.dtype)


def correlate(plan, scalars, before, lo, hi, after, delay, extra, parts):
    tile_first, is_first, is_last = plan
    segs, half, columns = lo.shape
    chans = 2 * half
    tiles = columns // (2 * TILE)
    slots = scalars.shape[0] - 1
    lags = delay.shape[2]
    keep = lags // parts
    spec = pl.BlockSpec((segs, half, 2 * TILE), lambda j, s: (0, 0, j))
    flat = pl.BlockSpec((slots * chans, lags), lambda j, s: (0, 0))
    vector = pl.BlockSpec((1, chans), lambda j, s: (0, 0))
    frame = lambda width: pl.BlockSpec((slots, 3 * half, width), lambda j, s: (0, 0, 0))
    scratch = [
        pltpu.VMEM((slots * chans, 2 * chans), jnp.bfloat16),
        pltpu.VMEM((segs, 2 * chans, 2 * TILE), jnp.bfloat16),
        pltpu.VMEM((segs, slots * chans, 2 * TILE), jnp.float32),
        pltpu.VMEM((slots * chans, 2 * TILE), jnp.bfloat16),
    ]
    out_shape, out_specs = [], []
    if is_last:
        out_shape += [
            jax.ShapeDtypeStruct((slots, 3 * half, keep), jnp.float32),
            jax.ShapeDtypeStruct((slots, 3 * half, lags - keep), jnp.bfloat16),
        ]
        out_specs += [frame(keep), frame(lags - keep)]
        scratch = [pltpu.VMEM((slots * chans, lags), jnp.float32)] + scratch
    else:
        out_shape += [jax.ShapeDtypeStruct((slots * chans, lags), jnp.float32)]
        out_specs += [flat]
    if is_first:
        out_shape += [jax.ShapeDtypeStruct((slots, chans, TILE), jnp.float32)]
        out_specs += [pl.BlockSpec((slots, chans, TILE), lambda j, s: (0, 0, 0))]
    return pl.pallas_call(
        functools.partial(correlate_kernel, plan),
        out_shape=out_shape,
        grid_spec=pltpu.PrefetchScalarGridSpec(
            num_scalar_prefetch=1,
            grid=(tiles,),
            in_specs=[spec, spec, spec, spec]
            + [pl.BlockSpec((None, 2 * TILE, lags), lambda j, s: (s[0], tile_first + j, 0))]
            + ([vector, vector] if is_first else [flat]),
            out_specs=out_specs,
            scratch_shapes=scratch,
        ),
        compiler_params=pltpu.CompilerParams(vmem_limit_bytes=32 * MIB),
        cost_estimate=pl.CostEstimate(
            flops=tiles * 2 * slots * chans * 2 * TILE * (segs * 2 * chans + lags),
            bytes_accessed=tiles * (4 * segs * half * 2 * TILE * 2),
            transcendentals=0,
        ),
        name="correlate",
    )(scalars, before, lo, hi, after, delay, *extra)


def gather_kernel(scalars, keep_ref, got_ref, mine_ref, other_ref, back_ref):
    _, rows, _ = mine_ref.shape
    half = back_ref.shape[1]
    back_ref[...] = (keep_ref[:, :half] + got_ref[:, :half].astype(jnp.float32)).astype(back_ref.dtype)
    mine = pl.ds(pl.multiple_of(half + scalars[0] * rows, rows), rows)
    other = pl.ds(pl.multiple_of(half + (1 - scalars[0]) * rows, rows), rows)
    mine_ref[...] = keep_ref[:, mine, :] + got_ref[:, mine, :].astype(jnp.float32)
    other_ref[...] = (keep_ref[:, other, :] + got_ref[:, other, :].astype(jnp.float32)).astype(other_ref.dtype)


def gather(span, keep, got):
    slots, rows, lags = keep.shape
    half = rows // 3
    spec = lambda r: pl.BlockSpec((slots, r, lags), lambda j, s: (0, 0, 0))
    return pl.pallas_call(
        gather_kernel,
        out_shape=[
            jax.ShapeDtypeStruct((slots, half, lags), jnp.float32),
            jax.ShapeDtypeStruct((slots, half, lags), jnp.bfloat16),
            jax.ShapeDtypeStruct((slots, half, lags), jnp.bfloat16),
        ],
        grid_spec=pltpu.PrefetchScalarGridSpec(
            num_scalar_prefetch=1, grid=(1,), in_specs=[spec(rows)] * 2, out_specs=[spec(half)] * 3
        ),
        name="gather",
    )(span, keep, got)


def finish_kernel(scalars, mine_ref, other_ref, near_ref, far_ref, inverse_ref, out_ref):
    slots, rows, lags = mine_ref.shape
    mine = pl.ds(pl.multiple_of(scalars[0] * rows, rows), rows)
    for slot in range(slots):
        scale = inverse_ref[slot, mine, :]
        scale = jnp.concatenate([scale] * (lags // TILE), axis=1)
        block = mine_ref[slot] + other_ref[slot].astype(jnp.float32)
        block += near_ref[slot].astype(jnp.float32) + far_ref[slot].astype(jnp.float32)
        out_ref[slot] = block * scale


def finish(span, mine, other, near, far, inverse):
    slots, rows, lags = mine.shape
    spec = pl.BlockSpec((slots, rows, lags), lambda j, s: (0, 0, 0))
    return pl.pallas_call(
        finish_kernel,
        out_shape=jax.ShapeDtypeStruct((slots, rows, lags), jnp.float32),
        grid_spec=pltpu.PrefetchScalarGridSpec(
            num_scalar_prefetch=1,
            grid=(1,),
            in_specs=[spec] * 4 + [pl.BlockSpec(inverse.shape, lambda j, s: (0, 0, 0))],
            out_specs=spec,
        ),
        name="finish",
    )(span, mine, other, near, far, inverse)


def shift(block, axis, distance):
    devices = range(lax.axis_size(axis))
    return lax.ppermute(block, axis, [(i, i + distance) for i in devices if i + distance in devices])


def reduced(span, keep, got, chans):
    spans = lax.axis_size("seg")
    half = chans // 2
    keep = keep + got.astype(jnp.float32)
    back = shift(keep[:, :half].astype(jnp.bfloat16), "chan", -1).astype(jnp.float32)
    keep = keep[:, half:] + jnp.pad(back, ((0, 0), (chans - half, 0), (0, 0)))
    piece = chans // spans
    result = lax.dynamic_slice_in_dim(keep, span * piece, piece, 1)
    for step in range(1, spans):
        target = lax.rem(span + step, spans)
        block = lax.dynamic_slice_in_dim(keep, target * piece, piece, 1).astype(jnp.bfloat16)
        block = lax.ppermute(block, "seg", [(i, (i + step) % spans) for i in range(spans)])
        result = result + block.astype(jnp.float32)
    return result


def shards(traces, dead_mask, seg_counts, offsets):
    segs, chans, length = traces.shape
    parts, spans, blocks = lax.axis_size("freq"), lax.axis_size("seg"), lax.axis_size("chan")
    assert parts == 2
    fourier, delay, band = (jnp.asarray(table) for table in tables(length, parts))
    tiles = fourier.shape[1] - 1
    part = lax.axis_index("freq").astype(jnp.int32)
    span = lax.axis_index("seg").astype(jnp.int32)
    counts, alive = seg_counts.reshape(1, chans), dead_mask.reshape(1, chans)
    next_counts = shift(seg_counts, "chan", -1).reshape(1, chans)
    rows = traces.reshape(segs * chans, length)
    place = jnp.stack([part, span * segs])
    scalars = jnp.concatenate([part.reshape(1), offsets])

    blocks_out, carried = [], []
    made = 0
    for index, stop in enumerate(GROUPS):
        plan = ((made, stop), (max(made - 1, 1), stop - 1 if stop <= tiles else tiles + 1), tiles)
        lo, hi, *carried = whiten(plan, place, rows, fourier, band, counts, alive, carried, segs)
        up, down = hi, lo
        if blocks_out:
            up, down, *earlier = lax.optimization_barrier((up, down, blocks_out[-1][0], blocks_out[-1][3]))
            blocks_out[-1] = (earlier[0], *blocks_out[-1][1:3], earlier[1])
        blocks_out.append((shift(up, "chan", 1), lo, hi, shift(down, "chan", -1)))
        made = stop
    extra, tile_first = [counts, next_counts], 0
    for index, group in enumerate(blocks_out):
        plan = (tile_first, index == 0, index == len(blocks_out) - 1)
        results = list(correlate(plan, scalars, *group, delay, extra, parts))
        if index == 0:
            inverse = results.pop()
        extra = results
        tile_first += group[1].shape[2] // (2 * TILE)
    keep, send = results
    got = lax.ppermute(send, "freq", [(0, 1), (1, 0)])
    if spans == 2:
        position = span.reshape(1)
        mine, other, back = gather(position, keep, got)
        other = lax.ppermute(other, "seg", [(0, 1), (1, 0)])
        near = lax.ppermute(back, ("chan", "seg"), [(2 * i + 3, 2 * i + 1) for i in range(blocks - 1)])
        far = lax.ppermute(back, ("chan", "seg"), [(2 * i + 2, 2 * i + 1) for i in range(blocks - 1)])
        result = finish(position, mine, other, near, far, inverse)
    else:
        piece = chans // spans
        result = reduced(span, keep, got, chans)
        result = result * lax.dynamic_slice_in_dim(inverse, span * piece, piece, 1)[:, :, :1]
    return jnp.transpose(result, (1, 0, 2))


def solution(mesh):
    in_specs = (
        P("seg", ("groups", "chan"), None),
        P(("groups", "chan")),
        P(("groups", "chan")),
        P(),
    )
    out_specs = P(("groups", "chan", "seg"), None, "freq")
    return jax.shard_map(shards, mesh=mesh, in_specs=in_specs, out_specs=out_specs, check_vma=False)
```

```python
import functools
import math

import jax
import jax.numpy as jnp
import numpy as np
from jax import lax
from jax.experimental import pallas as pl
from jax.experimental.pallas import tpu as pltpu
from jax.sharding import PartitionSpec as P
import ml_dtypes

HALF = 32
LAGS = 512
F = 2048
TILE = 128
EPSILON = 1e-06
MIB = 1 << 20
GROUPS = (5, 9)


def tables(length, parts):
    bins_dev = F // parts
    tiles = bins_dev // TILE
    cosines = np.cos(np.arange(length) * (2.0 * math.pi / length))
    sines = -np.sin(np.arange(length) * (2.0 * math.pi / length))
    cos16 = cosines.astype(np.float32).astype(ml_dtypes.bfloat16)
    sin16 = sines.astype(np.float32).astype(ml_dtypes.bfloat16)
    samples = np.arange(length)[:, None]
    fourier = np.zeros((parts, tiles + 1, length, 2 * TILE), ml_dtypes.bfloat16)
    for part in range(parts):
        for tile in range(tiles + 1):
            first = part * bins_dev + (tile - 1) * TILE
            bin_index = first + np.arange(TILE)
            keep = np.ones((TILE,), bool)
            if tile == 0:
                lane = np.arange(TILE)
                after = part * bins_dev + bins_dev + lane
                before = part * bins_dev - TILE + lane
                bin_index = np.where(lane < HALF, after, before)
                keep = ((lane < HALF) & (after < F)) | ((lane >= TILE - HALF) & (before >= 0))
            phases = samples * bin_index[None, :] % length
            zero = ml_dtypes.bfloat16(0)
            fourier[part, tile, :, :TILE] = np.where(keep, cos16[phases], zero)
            fourier[part, tile, :, TILE:] = np.where(keep, sin16[phases], zero)
    lag_part = LAGS // parts
    delay = np.zeros((parts, 2 * bins_dev, LAGS), ml_dtypes.bfloat16)
    scaling = 1.0 / math.sqrt(F)
    for part in range(parts):
        shifts = np.roll(np.arange(LAGS), -part * lag_part) - LAGS // 2
        for tile in range(tiles):
            bin_index = part * bins_dev + tile * TILE + np.arange(TILE)
            phases = bin_index[:, None] * shifts[None, :] % length
            rows = tile * 2 * TILE
            delay[part, rows : rows + TILE] = (cosines[phases] * scaling).astype(ml_dtypes.bfloat16)
            delay[part, rows + TILE : rows + 2 * TILE] = (sines[phases] * scaling).astype(ml_dtypes.bfloat16)
    return fourier, delay


def whiten_kernel(plan, scalars, table_ref, *refs):
    (first, stop), _, tiles = plan
    refs = list(refs)
    x, limits = refs.pop(0), refs.pop(0)
    if first:
        carried_spectrum, carried_power = refs.pop(0), refs.pop(0)
    one_ref, two_ref = refs.pop(0), refs.pop(0)
    handed = stop <= tiles
    if handed:
        handed_spectrum, handed_power = refs.pop(0), refs.pop(0)
    spectra, power, band, eff = refs
    step = pl.program_id(0)
    made = stop - first
    segs, half, _ = one_ref.shape
    chans = 2 * half
    edge = 0 if first else 3
    lag = 1 if first else 3
    even = scalars[2] == 0

    def store():
        block = jnp.dot(x[...], table_ref[...], preferred_element_type=jnp.float32)
        slot = step + 1
        spectra[slot] = block
        re, im = block[:, :TILE], block[:, TILE:]
        power[slot + 2] = (re * re + im * im).astype(jnp.bfloat16)

    def finish():
        tile = first + step - 2
        slot = step - 1
        before, after = slot + 1, jnp.where(tile == tiles, edge, slot + 3)
        window = jnp.dot(power[before], band[:TILE], preferred_element_type=jnp.float32)
        window += jnp.dot(power[slot + 2], band[TILE : 2 * TILE], preferred_element_type=jnp.float32)
        window += jnp.dot(power[after], band[2 * TILE :], preferred_element_type=jnp.float32)
        bin_index = scalars[0] * (tiles * TILE) + (tile - 1) * TILE + lax.broadcasted_iota(jnp.int32, (1, TILE), 1)
        count = jnp.minimum(bin_index + HALF, F - 1) - jnp.maximum(bin_index - HALF, 0) + 1
        inverse = 1.0 / count.astype(jnp.float32)
        for seg in range(segs):
            row = seg * chans
            scale = lax.rsqrt(window[row : row + chans] * inverse + EPSILON)
            number = (scalars[1] + seg).astype(jnp.float32)
            scale = jnp.where(number < eff[...], scale, 0.0)
            for lanes in (slice(0, TILE), slice(TILE, 2 * TILE)):
                white = spectra[slot, row : row + chans, lanes] * scale
                lo, hi = white[:half], white[half:]
                one_ref[seg, :, lanes] = jnp.where(even, hi, lo).astype(jnp.bfloat16)
                two_ref[seg, :, lanes] = jnp.where(even, lo, hi).astype(jnp.bfloat16)

    @pl.when(step == 0)
    def _():
        row = lax.broadcasted_iota(jnp.int32, (3 * TILE, TILE), 0)
        column = lax.broadcasted_iota(jnp.int32, (3 * TILE, TILE), 1)
        near = jnp.abs(row - TILE - column) <= HALF
        band[...] = near.astype(jnp.float32).astype(jnp.bfloat16)
        eff[...] = jnp.transpose(jnp.broadcast_to(limits[...], (chans, chans)))
        if first:
            spectra[0] = carried_spectrum[...]
            power[0:3] = carried_power[...]

    @pl.when(step < lag)
    def _():
        store()

    @pl.when((step >= lag) & (step < made))
    def _():
        finish()
        store()

    @pl.when(step >= made)
    def _():
        finish()

    if handed:

        @pl.when(step == made)
        def _():
            handed_spectrum[...] = spectra[made]
            handed_power[0] = power[edge]
            handed_power[1] = power[made + 1]
            handed_power[2] = power[made + 2]


def whiten(plan, scalars, operands, fourier, segs, chans):
    (first, stop), (done_first, done_stop), tiles = plan
    made, done = stop - first, done_stop - done_first
    half, total, length = chans // 2, segs * chans, fourier.shape[2]
    lag = 1 if first else 3
    out = jax.ShapeDtypeStruct((segs, half, 2 * TILE * done), jnp.bfloat16)
    out_spec = pl.BlockSpec((segs, half, 2 * TILE), lambda j, p: (0, 0, jnp.clip(j - lag, 0, done - 1)))
    out_shape, out_specs = [out, out], [out_spec, out_spec]
    scratch = [
        pltpu.VMEM((made + 1, total, 2 * TILE), jnp.float32),
        pltpu.VMEM((made + 3, total, TILE), jnp.bfloat16),
        pltpu.VMEM((3 * TILE, TILE), jnp.bfloat16),
        pltpu.VMEM((chans, chans), jnp.float32),
    ]
    here = pl.BlockSpec(memory_space=pltpu.VMEM)
    if stop <= tiles:
        out_shape += [
            jax.ShapeDtypeStruct((total, 2 * TILE), jnp.float32),
            jax.ShapeDtypeStruct((3, total, TILE), jnp.bfloat16),
        ]
        out_specs += [here, here]
    return pl.pallas_call(
        functools.partial(whiten_kernel, plan),
        out_shape=out_shape,
        grid_spec=pltpu.PrefetchScalarGridSpec(
            num_scalar_prefetch=1,
            grid=(done + lag,),
            in_specs=[
                pl.BlockSpec(
                    (None, None, length, 2 * TILE), lambda j, p: (p[0], jnp.minimum(first + j, stop - 1), 0, 0)
                ),
            ]
            + [here] * len(operands),
            out_specs=out_specs,
            scratch_shapes=scratch,
        ),
        compiler_params=pltpu.CompilerParams(vmem_limit_bytes=36 * MIB),
        cost_estimate=pl.CostEstimate(
            flops=2 * total * length * 2 * TILE * made,
            bytes_accessed=2 * length * 2 * TILE * made + 2 * total * length,
            transcendentals=0,
        ),
        name="whiten",
    )(scalars, fourier, *operands)


def window_start(offset, chans):
    return jnp.minimum(chans // 2, chans - offset) // 16 * 16


def correlate_kernel(plan, scalars, one_ref, two_ref, got_one_ref, got_two_ref, delay_ref, *refs):
    tile_first, is_first, is_last = plan
    refs = list(refs)
    if is_first:
        own_counts, next_counts = refs.pop(0), refs.pop(0)
    else:
        sum_ref = refs.pop(0)
    if is_last:
        keep_ref, send_ref = refs.pop(0), refs.pop(0)
    else:
        total = refs.pop(0)
    if is_first:
        inverse_ref = refs.pop(0)
    if is_last:
        total = refs.pop(0)
    select, frame, far, cross = refs
    step, last = pl.program_id(0), pl.num_programs(0) - 1
    segs, half, _ = one_ref.shape
    chans = 2 * half
    slots = cross.shape[0] // chans
    even, known = scalars[1] == 0, scalars[2]

    @pl.when(step == 0)
    def _():
        total[...] = jnp.zeros_like(total) if is_first else sum_ref[...]
        row = lax.broadcasted_iota(jnp.int32, (chans, 2 * chans), 0)
        column = lax.broadcasted_iota(jnp.int32, (chans, 2 * chans), 1)
        for slot in range(slots):
            offset = scalars[3 + slot]
            match = (column == row + window_start(offset, chans) + offset) & (column < known)
            select[slot * chans : (slot + 1) * chans] = match.astype(jnp.float32).astype(jnp.bfloat16)
        if is_first:
            row = lax.broadcasted_iota(jnp.int32, (chans, chans), 0)
            column = lax.broadcasted_iota(jnp.int32, (chans, chans), 1)
            own, following = own_counts[...].astype(jnp.float32), next_counts[...].astype(jnp.float32)
            mine = jnp.sum(jnp.where(row == column, own, 0.0), axis=1, keepdims=True)
            for slot in range(slots):
                target = row + scalars[3 + slot]
                partner = jnp.where(column == target, own, 0.0) + jnp.where(column + chans == target, following, 0.0)
                partner = jnp.sum(partner, axis=1, keepdims=True)
                divisor = jnp.maximum(jnp.minimum(mine, partner), 1.0)
                inverse_ref[slot] = jnp.broadcast_to(1.0 / divisor, inverse_ref.shape[1:])

    order = ((one_ref, 2, 1), (two_ref, 1, 2), (got_one_ref, 3, 0), (got_two_ref, 0, 3))
    for ref, if_even, if_odd in order:
        spot = pl.ds(pl.multiple_of(jnp.where(even, if_even * half, if_odd * half), half), half)
        for seg in range(segs):
            frame[seg, spot, :] = ref[seg]
    for seg in range(segs):
        far[seg] = jnp.dot(select[...], frame[seg], preferred_element_type=jnp.float32)
    for slot in range(slots):
        start = window_start(scalars[3 + slot], chans)

        def rows(index, carry, slot=slot, start=start):
            real = jnp.zeros((16, TILE), jnp.float32)
            imag = jnp.zeros((16, TILE), jnp.float32)
            base = pl.multiple_of(start + index * 16, 16)
            spot = pl.multiple_of(slot * chans + index * 16, 16)
            for seg in range(segs):
                own = frame[seg, pl.ds(base, 16), :].astype(jnp.float32)
                own_re, own_im = own[:, :TILE], own[:, TILE:]
                far_re, far_im = far[seg, pl.ds(spot, 16), :TILE], far[seg, pl.ds(spot, 16), TILE:]
                real += own_re * far_re + own_im * far_im
                imag += own_im * far_re - own_re * far_im
            cross[pl.ds(spot, 16), :TILE] = real.astype(jnp.bfloat16)
            cross[pl.ds(spot, 16), TILE:] = imag.astype(jnp.bfloat16)
            return carry

        lax.fori_loop(0, chans // 16, rows, 0, unroll=True)
    total[...] += jnp.dot(cross[...], delay_ref[...], preferred_element_type=jnp.float32)

    if is_last:

        @pl.when(step == last)
        def _():
            keep = keep_ref.shape[2]
            keep_ref[...] = jnp.zeros_like(keep_ref)
            send_ref[...] = jnp.zeros_like(send_ref)
            for slot in range(slots):
                start = pl.multiple_of(window_start(scalars[3 + slot], chans), 16)
                block = total[slot * chans : (slot + 1) * chans]
                keep_ref[slot, pl.ds(start, chans), :] = block[:, :keep]
                send_ref[slot, pl.ds(start, chans), :] = block[:, keep:].astype(send_ref.dtype)


def correlate(plan, scalars, one, two, got_one, got_two, delay, extra, parts):
    tile_first, is_first, is_last = plan
    segs, half, columns = one.shape
    chans = 2 * half
    tiles = columns // (2 * TILE)
    slots = scalars.shape[0] - 3
    lags = delay.shape[2]
    keep = lags // parts
    spec = pl.BlockSpec((segs, half, 2 * TILE), lambda j, s: (0, 0, j))
    flat = pl.BlockSpec(memory_space=pltpu.VMEM)
    vector = pl.BlockSpec((1, chans), lambda j, s: (0, 0))
    frame = lambda width: pl.BlockSpec((slots, 3 * half, width), lambda j, s: (0, 0, 0))
    scratch = [
        pltpu.VMEM((slots * chans, 2 * chans), jnp.bfloat16),
        pltpu.VMEM((segs, 2 * chans, 2 * TILE), jnp.bfloat16),
        pltpu.VMEM((segs, slots * chans, 2 * TILE), jnp.float32),
        pltpu.VMEM((slots * chans, 2 * TILE), jnp.bfloat16),
    ]
    out_shape, out_specs = [], []
    if is_last:
        out_shape += [
            jax.ShapeDtypeStruct((slots, 3 * half, keep), jnp.float32),
            jax.ShapeDtypeStruct((slots, 3 * half, lags - keep), jnp.bfloat16),
        ]
        out_specs += [frame(keep), frame(lags - keep)]
        scratch = [pltpu.VMEM((slots * chans, lags), jnp.float32)] + scratch
    else:
        out_shape += [jax.ShapeDtypeStruct((slots * chans, lags), jnp.float32)]
        out_specs += [flat]
    if is_first:
        out_shape += [jax.ShapeDtypeStruct((slots, chans, keep), jnp.float32)]
        out_specs += [flat]
    return pl.pallas_call(
        functools.partial(correlate_kernel, plan),
        out_shape=out_shape,
        grid_spec=pltpu.PrefetchScalarGridSpec(
            num_scalar_prefetch=1,
            grid=(tiles,),
            in_specs=[spec, spec, spec, spec]
            + [pl.BlockSpec((None, 2 * TILE, lags), lambda j, s: (s[0], tile_first + j, 0))]
            + ([vector, vector] if is_first else [flat]),
            out_specs=out_specs,
            scratch_shapes=scratch,
        ),
        compiler_params=pltpu.CompilerParams(vmem_limit_bytes=32 * MIB),
        cost_estimate=pl.CostEstimate(
            flops=tiles * 2 * slots * chans * 2 * TILE * (segs * 2 * chans + lags),
            bytes_accessed=tiles * (4 * segs * half * 2 * TILE * 2),
            transcendentals=0,
        ),
        name="correlate",
    )(scalars, one, two, got_one, got_two, delay, *extra)


def neighbours(devices, first):
    route = list(range(devices))
    for i in range(first, devices - 1, 2):
        route[i], route[i + 1] = i + 1, i
    return list(enumerate(route))


def reduced(span, keep, chans, has_next):
    spans, blocks = lax.axis_size("seg"), lax.axis_size("chan")
    half = chans // 2
    back = lax.ppermute(keep[:, :half].astype(jnp.bfloat16), "chan", [(i, (i - 1) % blocks) for i in range(blocks)])
    back = jnp.where(has_next, back.astype(jnp.float32), 0.0)
    keep = keep[:, half:] + jnp.pad(back, ((0, 0), (chans - half, 0), (0, 0)))
    piece = chans // spans
    result = lax.dynamic_slice_in_dim(keep, span * piece, piece, 1)
    for step in range(1, spans):
        target = lax.rem(span + step, spans)
        block = lax.dynamic_slice_in_dim(keep, target * piece, piece, 1).astype(jnp.bfloat16)
        block = lax.ppermute(block, "seg", [(i, (i + step) % spans) for i in range(spans)])
        result = result + block.astype(jnp.float32)
    return result


def shards(traces, dead_mask, seg_counts, offsets):
    segs, chans, length = traces.shape
    half = chans // 2
    parts, spans, blocks = lax.axis_size("freq"), lax.axis_size("seg"), lax.axis_size("chan")
    assert parts == 2
    fourier, delay = (jnp.asarray(table) for table in tables(length, parts))
    tiles = fourier.shape[1] - 1
    part = lax.axis_index("freq").astype(jnp.int32)
    span = lax.axis_index("seg").astype(jnp.int32)
    place = lax.axis_index("chan").astype(jnp.int32)
    has_next = place < blocks - 1
    counts = seg_counts.reshape(1, chans)
    limits = jnp.where(dead_mask > 0, seg_counts, 0).astype(jnp.float32).reshape(1, chans)
    next_counts = lax.ppermute(seg_counts, "chan", [(i, (i - 1) % blocks) for i in range(blocks)]).reshape(1, chans)
    parity = place & 1
    scalars = jnp.stack([part, span * segs, parity])
    known = jnp.where(has_next, 4 * half, 3 * half)
    settings = jnp.concatenate([jnp.stack([part, parity, known]), offsets])

    groups, operands, made = [], [traces.reshape(segs * chans, length), limits], 0
    for stop in GROUPS:
        plan = ((made, stop), (max(made - 1, 1), stop - 1 if stop <= tiles else tiles + 1), tiles)
        one, two, *passed = whiten(plan, scalars, operands, fourier, segs, chans)
        operands = operands[:2] + passed
        send_one, send_two = one, two
        if groups:
            send_one, send_two, *earlier = lax.optimization_barrier((one, two, *groups[-1][2:]))
            groups[-1] = (*groups[-1][:2], *earlier)
        got_one = lax.ppermute(send_one, "chan", neighbours(blocks, 0))
        got_two = lax.ppermute(send_two, "chan", neighbours(blocks, 1))
        groups.append((one, two, got_one, got_two))
        made = stop
    extra, tile_first = [counts, next_counts], 0
    for index, group in enumerate(groups):
        plan = (tile_first, index == 0, index == len(groups) - 1)
        results = list(correlate(plan, settings, *group, delay, extra, parts))
        if index == 0:
            inverse = results.pop()
        extra = results
        tile_first += group[0].shape[2] // (2 * TILE)
    keep, send = results
    keep = keep + lax.ppermute(send, "freq", [(0, 1), (1, 0)]).astype(jnp.float32)
    if spans == 2:
        lower, upper = keep[:, half:chans], keep[:, chans:]
        mine = jnp.where(span == 0, lower, upper)
        other = jnp.where(span == 0, upper, lower).astype(jnp.bfloat16)
        back = keep[:, :half].astype(jnp.bfloat16)
        other = lax.ppermute(other, "seg", [(0, 1), (1, 0)])
        route = [(2 * i + 1, 2 * ((i - 1) % blocks) + 1) for i in range(blocks)]
        near = lax.ppermute(back, ("chan", "seg"), route + [(2 * i, 2 * i) for i in range(blocks)])
        route = [(2 * i, 2 * ((i - 1) % blocks) + 1) for i in range(blocks)]
        far = lax.ppermute(back, ("chan", "seg"), route + [(2 * i + 1, 2 * i) for i in range(blocks)])
        returned = jnp.where(has_next & (span == 1), near.astype(jnp.float32) + far.astype(jnp.float32), 0.0)
        result = mine + other.astype(jnp.float32) + returned
        result = result * jnp.where(span == 0, inverse[:, :half], inverse[:, half:])
    else:
        piece = chans // spans
        result = reduced(span, keep, chans, has_next)
        result = result * lax.dynamic_slice_in_dim(inverse, span * piece, piece, 1)
    return jnp.transpose(result, (1, 0, 2))


def solution(mesh):
    in_specs = (
        P("seg", ("groups", "chan"), None),
        P(("groups", "chan")),
        P(("groups", "chan")),
        P(),
    )
    out_specs = P(("groups", "chan", "seg"), None, "freq")
    return jax.shard_map(shards, mesh=mesh, in_specs=in_specs, out_specs=out_specs, check_vma=False)
```

```python
import functools
import math

import jax
import jax.numpy as jnp
import numpy as np
from jax import lax
from jax.experimental import pallas as pl
from jax.experimental.pallas import tpu as pltpu
from jax.sharding import PartitionSpec as P
import ml_dtypes

HALF = 32
LAGS = 512
F = 2048
TILE = 128
EPSILON = 1e-06
MIB = 1 << 20
GROUPS = (6, 9)


def tables(length, parts):
    bins_dev = F // parts
    tiles = bins_dev // TILE
    cosines = np.cos(np.arange(length) * (2.0 * math.pi / length))
    sines = -np.sin(np.arange(length) * (2.0 * math.pi / length))
    cos16 = cosines.astype(np.float32).astype(ml_dtypes.bfloat16)
    sin16 = sines.astype(np.float32).astype(ml_dtypes.bfloat16)
    samples = np.arange(length)[:, None]
    fourier = np.zeros((parts, tiles + 1, length, 2 * TILE), ml_dtypes.bfloat16)
    for part in range(parts):
        for tile in range(tiles + 1):
            first = part * bins_dev + (tile - 1) * TILE
            bin_index = first + np.arange(TILE)
            keep = np.ones((TILE,), bool)
            if tile == 0:
                lane = np.arange(TILE)
                after = part * bins_dev + bins_dev + lane
                before = part * bins_dev - TILE + lane
                bin_index = np.where(lane < HALF, after, before)
                keep = ((lane < HALF) & (after < F)) | ((lane >= TILE - HALF) & (before >= 0))
            phases = samples * bin_index[None, :] % length
            zero = ml_dtypes.bfloat16(0)
            fourier[part, tile, :, :TILE] = np.where(keep, cos16[phases], zero)
            fourier[part, tile, :, TILE:] = np.where(keep, sin16[phases], zero)
    lag_part = LAGS // parts
    delay = np.zeros((parts, 2 * bins_dev, LAGS), ml_dtypes.bfloat16)
    scaling = 1.0 / math.sqrt(F)
    for part in range(parts):
        shifts = np.roll(np.arange(LAGS), -part * lag_part) - LAGS // 2
        for tile in range(tiles):
            bin_index = part * bins_dev + tile * TILE + np.arange(TILE)
            phases = bin_index[:, None] * shifts[None, :] % length
            rows = tile * 2 * TILE
            delay[part, rows : rows + TILE] = (cosines[phases] * scaling).astype(ml_dtypes.bfloat16)
            delay[part, rows + TILE : rows + 2 * TILE] = (sines[phases] * scaling).astype(ml_dtypes.bfloat16)
    return fourier, delay


def whiten_kernel(plan, scalars, table_ref, *refs):
    (first, stop), _, tiles = plan
    refs = list(refs)
    x, limits = refs.pop(0), refs.pop(0)
    if first:
        carried_spectrum, carried_power = refs.pop(0), refs.pop(0)
    one_ref, two_ref = refs.pop(0), refs.pop(0)
    handed = stop <= tiles
    if handed:
        handed_spectrum, handed_power = refs.pop(0), refs.pop(0)
    spectra, power, band, eff = refs
    step = pl.program_id(0)
    made = stop - first
    segs, half, _ = one_ref.shape
    chans = 2 * half
    edge = 0 if first else 3
    lag = 1 if first else 3
    even = scalars[2] == 0

    def store():
        block = jnp.dot(x[...], table_ref[...], preferred_element_type=jnp.float32)
        slot = step + 1
        spectra[slot] = block
        re, im = block[:, :TILE], block[:, TILE:]
        power[slot + 2] = (re * re + im * im).astype(jnp.bfloat16)

    def finish():
        tile = first + step - 2
        slot = step - 1
        before, after = slot + 1, jnp.where(tile == tiles, edge, slot + 3)
        window = jnp.dot(power[before], band[:TILE], preferred_element_type=jnp.float32)
        window += jnp.dot(power[slot + 2], band[TILE : 2 * TILE], preferred_element_type=jnp.float32)
        window += jnp.dot(power[after], band[2 * TILE :], preferred_element_type=jnp.float32)
        bin_index = scalars[0] * (tiles * TILE) + (tile - 1) * TILE + lax.broadcasted_iota(jnp.int32, (1, TILE), 1)
        count = jnp.minimum(bin_index + HALF, F - 1) - jnp.maximum(bin_index - HALF, 0) + 1
        inverse = 1.0 / count.astype(jnp.float32)
        for seg in range(segs):
            row = seg * chans
            scale = lax.rsqrt(window[row : row + chans] * inverse + EPSILON)
            number = (scalars[1] + seg).astype(jnp.float32)
            scale = jnp.where(number < eff[...], scale, 0.0)
            for lanes in (slice(0, TILE), slice(TILE, 2 * TILE)):
                white = spectra[slot, row : row + chans, lanes] * scale
                lo, hi = white[:half], white[half:]
                one_ref[seg, :, lanes] = jnp.where(even, hi, lo).astype(jnp.bfloat16)
                two_ref[seg, :, lanes] = jnp.where(even, lo, hi).astype(jnp.bfloat16)

    @pl.when(step == 0)
    def _():
        row = lax.broadcasted_iota(jnp.int32, (3 * TILE, TILE), 0)
        column = lax.broadcasted_iota(jnp.int32, (3 * TILE, TILE), 1)
        near = jnp.abs(row - TILE - column) <= HALF
        band[...] = near.astype(jnp.float32).astype(jnp.bfloat16)
        eff[...] = jnp.transpose(jnp.broadcast_to(limits[...], (chans, chans)))
        if first:
            spectra[0] = carried_spectrum[...]
            power[0:3] = carried_power[...]

    @pl.when(step < lag)
    def _():
        store()

    @pl.when((step >= lag) & (step < made))
    def _():
        finish()
        store()

    @pl.when(step >= made)
    def _():
        finish()

    if handed:

        @pl.when(step == made)
        def _():
            handed_spectrum[...] = spectra[made]
            handed_power[0] = power[edge]
            handed_power[1] = power[made + 1]
            handed_power[2] = power[made + 2]


def whiten(plan, scalars, operands, fourier, segs, chans):
    (first, stop), (done_first, done_stop), tiles = plan
    made, done = stop - first, done_stop - done_first
    half, total, length = chans // 2, segs * chans, fourier.shape[2]
    lag = 1 if first else 3
    out = jax.ShapeDtypeStruct((segs, half, 2 * TILE * done), jnp.bfloat16)
    out_spec = pl.BlockSpec((segs, half, 2 * TILE), lambda j, p: (0, 0, jnp.clip(j - lag, 0, done - 1)))
    out_shape, out_specs = [out, out], [out_spec, out_spec]
    scratch = [
        pltpu.VMEM((made + 1, total, 2 * TILE), jnp.float32),
        pltpu.VMEM((made + 3, total, TILE), jnp.bfloat16),
        pltpu.VMEM((3 * TILE, TILE), jnp.bfloat16),
        pltpu.VMEM((chans, chans), jnp.float32),
    ]
    here = pl.BlockSpec(memory_space=pltpu.VMEM)
    if stop <= tiles:
        out_shape += [
            jax.ShapeDtypeStruct((total, 2 * TILE), jnp.float32),
            jax.ShapeDtypeStruct((3, total, TILE), jnp.bfloat16),
        ]
        out_specs += [here, here]
    return pl.pallas_call(
        functools.partial(whiten_kernel, plan),
        out_shape=out_shape,
        grid_spec=pltpu.PrefetchScalarGridSpec(
            num_scalar_prefetch=1,
            grid=(done + lag,),
            in_specs=[
                pl.BlockSpec(
                    (None, None, length, 2 * TILE), lambda j, p: (p[0], jnp.minimum(first + j, stop - 1), 0, 0)
                ),
            ]
            + [here] * len(operands),
            out_specs=out_specs,
            scratch_shapes=scratch,
        ),
        compiler_params=pltpu.CompilerParams(vmem_limit_bytes=36 * MIB),
        cost_estimate=pl.CostEstimate(
            flops=2 * total * length * 2 * TILE * made,
            bytes_accessed=2 * length * 2 * TILE * made + 2 * total * length,
            transcendentals=0,
        ),
        name="whiten",
    )(scalars, fourier, *operands)


def window_start(offset, chans):
    return jnp.minimum(chans // 2, chans - offset) // 16 * 16


def correlate_kernel(plan, scalars, one_ref, two_ref, got_one_ref, got_two_ref, delay_ref, *refs):
    tile_first, is_first, is_last = plan
    refs = list(refs)
    if is_first:
        own_counts, next_counts = refs.pop(0), refs.pop(0)
    else:
        sum_ref = refs.pop(0)
    if is_last:
        keep_ref, send_ref = refs.pop(0), refs.pop(0)
    else:
        total = refs.pop(0)
    if is_first:
        inverse_ref = refs.pop(0)
    if is_last:
        total = refs.pop(0)
    select, frame, far, cross = refs
    step, last = pl.program_id(0), pl.num_programs(0) - 1
    segs, half, _ = one_ref.shape
    chans = 2 * half
    slots = cross.shape[0] // chans
    even, known = scalars[1] == 0, scalars[2]

    @pl.when(step == 0)
    def _():
        total[...] = jnp.zeros_like(total) if is_first else sum_ref[...]
        row = lax.broadcasted_iota(jnp.int32, (chans, 2 * chans), 0)
        column = lax.broadcasted_iota(jnp.int32, (chans, 2 * chans), 1)
        for slot in range(slots):
            offset = scalars[3 + slot]
            match = (column == row + window_start(offset, chans) + offset) & (column < known)
            select[slot * chans : (slot + 1) * chans] = match.astype(jnp.float32).astype(jnp.bfloat16)
        if is_first:
            row = lax.broadcasted_iota(jnp.int32, (chans, chans), 0)
            column = lax.broadcasted_iota(jnp.int32, (chans, chans), 1)
            own, following = own_counts[...].astype(jnp.float32), next_counts[...].astype(jnp.float32)
            mine = jnp.sum(jnp.where(row == column, own, 0.0), axis=1, keepdims=True)
            for slot in range(slots):
                target = row + scalars[3 + slot]
                partner = jnp.where(column == target, own, 0.0) + jnp.where(column + chans == target, following, 0.0)
                partner = jnp.sum(partner, axis=1, keepdims=True)
                divisor = jnp.maximum(jnp.minimum(mine, partner), 1.0)
                inverse_ref[slot] = jnp.broadcast_to(1.0 / divisor, inverse_ref.shape[1:])

    order = ((one_ref, 2, 1), (two_ref, 1, 2), (got_one_ref, 3, 0), (got_two_ref, 0, 3))
    for ref, if_even, if_odd in order:
        spot = pl.ds(pl.multiple_of(jnp.where(even, if_even * half, if_odd * half), half), half)
        for seg in range(segs):
            frame[seg, spot, :] = ref[seg]
    for seg in range(segs):
        far[seg] = jnp.dot(select[...], frame[seg], preferred_element_type=jnp.float32)
    for slot in range(slots):
        start = window_start(scalars[3 + slot], chans)

        def rows(index, carry, slot=slot, start=start):
            real = jnp.zeros((16, TILE), jnp.float32)
            imag = jnp.zeros((16, TILE), jnp.float32)
            base = pl.multiple_of(start + index * 16, 16)
            spot = pl.multiple_of(slot * chans + index * 16, 16)
            for seg in range(segs):
                own = frame[seg, pl.ds(base, 16), :].astype(jnp.float32)
                own_re, own_im = own[:, :TILE], own[:, TILE:]
                far_re, far_im = far[seg, pl.ds(spot, 16), :TILE], far[seg, pl.ds(spot, 16), TILE:]
                real += own_re * far_re + own_im * far_im
                imag += own_im * far_re - own_re * far_im
            cross[pl.ds(spot, 16), :TILE] = real.astype(jnp.bfloat16)
            cross[pl.ds(spot, 16), TILE:] = imag.astype(jnp.bfloat16)
            return carry

        lax.fori_loop(0, chans // 16, rows, 0, unroll=True)
    total[...] += jnp.dot(cross[...], delay_ref[...], preferred_element_type=jnp.float32)

    if is_last:

        @pl.when(step == last)
        def _():
            keep = keep_ref.shape[2]
            keep_ref[...] = jnp.zeros_like(keep_ref)
            send_ref[...] = jnp.zeros_like(send_ref)
            for slot in range(slots):
                start = pl.multiple_of(window_start(scalars[3 + slot], chans), 16)
                block = total[slot * chans : (slot + 1) * chans]
                keep_ref[slot, pl.ds(start, chans), :] = block[:, :keep]
                send_ref[slot, pl.ds(start, chans), :] = block[:, keep:].astype(send_ref.dtype)


def correlate(plan, scalars, one, two, got_one, got_two, delay, extra, parts):
    tile_first, is_first, is_last = plan
    segs, half, columns = one.shape
    chans = 2 * half
    tiles = columns // (2 * TILE)
    slots = scalars.shape[0] - 3
    lags = delay.shape[2]
    keep = lags // parts
    spec = pl.BlockSpec((segs, half, 2 * TILE), lambda j, s: (0, 0, j))
    flat = pl.BlockSpec(memory_space=pltpu.VMEM)
    vector = pl.BlockSpec((1, chans), lambda j, s: (0, 0))
    frame = lambda width: pl.BlockSpec((slots, 3 * half, width), lambda j, s: (0, 0, 0))
    scratch = [
        pltpu.VMEM((slots * chans, 2 * chans), jnp.bfloat16),
        pltpu.VMEM((segs, 2 * chans, 2 * TILE), jnp.bfloat16),
        pltpu.VMEM((segs, slots * chans, 2 * TILE), jnp.float32),
        pltpu.VMEM((slots * chans, 2 * TILE), jnp.bfloat16),
    ]
    out_shape, out_specs = [], []
    if is_last:
        out_shape += [
            jax.ShapeDtypeStruct((slots, 3 * half, keep), jnp.float32),
            jax.ShapeDtypeStruct((slots, 3 * half, lags - keep), jnp.bfloat16),
        ]
        out_specs += [frame(keep), frame(lags - keep)]
        scratch = [pltpu.VMEM((slots * chans, lags), jnp.float32)] + scratch
    else:
        out_shape += [jax.ShapeDtypeStruct((slots * chans, lags), jnp.float32)]
        out_specs += [flat]
    if is_first:
        out_shape += [jax.ShapeDtypeStruct((slots, chans, keep), jnp.float32)]
        out_specs += [flat]
    return pl.pallas_call(
        functools.partial(correlate_kernel, plan),
        out_shape=out_shape,
        grid_spec=pltpu.PrefetchScalarGridSpec(
            num_scalar_prefetch=1,
            grid=(tiles,),
            in_specs=[spec, spec, spec, spec]
            + [pl.BlockSpec((None, 2 * TILE, lags), lambda j, s: (s[0], tile_first + j, 0))]
            + ([vector, vector] if is_first else [flat]),
            out_specs=out_specs,
            scratch_shapes=scratch,
        ),
        compiler_params=pltpu.CompilerParams(vmem_limit_bytes=32 * MIB),
        cost_estimate=pl.CostEstimate(
            flops=tiles * 2 * slots * chans * 2 * TILE * (segs * 2 * chans + lags),
            bytes_accessed=tiles * (4 * segs * half * 2 * TILE * 2),
            transcendentals=0,
        ),
        name="correlate",
    )(scalars, one, two, got_one, got_two, delay, *extra)


def swap(block, first):
    blocks, parts = lax.axis_size("chan"), lax.axis_size("freq")
    route = []
    for i in range(blocks):
        partner = i + 1 if (i - first) % 2 == 0 else i - 1
        alone = not 0 <= partner < blocks
        for part in range(parts):
            target = i * parts + (part + 1) % parts if alone else partner * parts + part
            route.append((i * parts + part, target))
    return lax.ppermute(block, ("chan", "freq"), route)


def returns(blocks, parts):
    near, far = {}, {}
    last = blocks - 1
    for i in range(blocks):
        near[i, 1] = (i - 1, 1) if i else (0, 0)
        near[i, 0] = (i + 1, 0) if i < last else (last, 1)
        far[i, 0] = (i - 1, 1) if i else (0, 0)
        far[i, 1] = (i + 1, 0) if i < last else (last, 1)
    routes = []
    for steps in (near, far):
        route = []
        for source, target in steps.items():
            for part in range(parts):
                end = (part + 1) % parts if source == target else part
                route.append(((2 * source[0] + source[1]) * parts + part, (2 * target[0] + target[1]) * parts + end))
        routes.append(route)
    return routes


def reduced(span, keep, chans, has_next):
    spans, blocks = lax.axis_size("seg"), lax.axis_size("chan")
    half = chans // 2
    back = lax.ppermute(keep[:, :half].astype(jnp.bfloat16), "chan", [(i, (i - 1) % blocks) for i in range(blocks)])
    back = jnp.where(has_next, back.astype(jnp.float32), 0.0)
    keep = keep[:, half:] + jnp.pad(back, ((0, 0), (chans - half, 0), (0, 0)))
    piece = chans // spans
    result = lax.dynamic_slice_in_dim(keep, span * piece, piece, 1)
    for step in range(1, spans):
        target = lax.rem(span + step, spans)
        block = lax.dynamic_slice_in_dim(keep, target * piece, piece, 1).astype(jnp.bfloat16)
        block = lax.ppermute(block, "seg", [(i, (i + step) % spans) for i in range(spans)])
        result = result + block.astype(jnp.float32)
    return result


def shards(traces, dead_mask, seg_counts, offsets):
    segs, chans, length = traces.shape
    half = chans // 2
    parts, spans, blocks = lax.axis_size("freq"), lax.axis_size("seg"), lax.axis_size("chan")
    assert parts == 2
    fourier, delay = (jnp.asarray(table) for table in tables(length, parts))
    tiles = fourier.shape[1] - 1
    part = lax.axis_index("freq").astype(jnp.int32)
    span = lax.axis_index("seg").astype(jnp.int32)
    place = lax.axis_index("chan").astype(jnp.int32)
    has_next = place < blocks - 1
    counts = seg_counts.reshape(1, chans)
    limits = jnp.where(dead_mask > 0, seg_counts, 0).astype(jnp.float32).reshape(1, chans)
    next_counts = lax.ppermute(seg_counts, "chan", [(i, (i - 1) % blocks) for i in range(blocks)]).reshape(1, chans)
    parity = place & 1
    scalars = jnp.stack([part, span * segs, parity])
    known = jnp.where(has_next, 4 * half, 3 * half)
    settings = jnp.concatenate([jnp.stack([part, parity, known]), offsets])

    groups, operands, made = [], [traces.reshape(segs * chans, length), limits], 0
    for stop in GROUPS:
        plan = ((made, stop), (max(made - 1, 1), stop - 1 if stop <= tiles else tiles + 1), tiles)
        one, two, *passed = whiten(plan, scalars, operands, fourier, segs, chans)
        operands = operands[:2] + passed
        if groups:
            send_one, send_two, *earlier = lax.optimization_barrier((one, two, *groups[-1][2:]))
            groups[-1] = (*groups[-1][:2], *earlier)
        else:
            send_one, send_two, next_counts = lax.optimization_barrier((one, two, next_counts))
        got_one, got_two = swap(send_one, 0), swap(send_two, 1)
        groups.append((one, two, got_one, got_two))
        made = stop
    extra, tile_first = [counts, next_counts], 0
    for index, group in enumerate(groups):
        plan = (tile_first, index == 0, index == len(groups) - 1)
        results = list(correlate(plan, settings, *group, delay, extra, parts))
        if index == 0:
            inverse = results.pop()
        extra = results
        tile_first += group[0].shape[2] // (2 * TILE)
    keep, send = results
    keep = keep + lax.ppermute(send, "freq", [(0, 1), (1, 0)]).astype(jnp.float32)
    if spans == 2:
        lower, upper = keep[:, half:chans], keep[:, chans:]
        mine = jnp.where(span == 0, lower, upper)
        other = jnp.where(span == 0, upper, lower).astype(jnp.bfloat16)
        back = keep[:, :half].astype(jnp.bfloat16)
        other = lax.ppermute(other, "seg", [(0, 1), (1, 0)])
        route_near, route_far = returns(blocks, parts)
        near = lax.ppermute(back, ("chan", "seg", "freq"), route_near)
        far = lax.ppermute(back, ("chan", "seg", "freq"), route_far)
        returned = jnp.where(has_next & (span == 1), near.astype(jnp.float32) + far.astype(jnp.float32), 0.0)
        result = mine + other.astype(jnp.float32) + returned
        result = result * jnp.where(span == 0, inverse[:, :half], inverse[:, half:])
    else:
        piece = chans // spans
        result = reduced(span, keep, chans, has_next)
        result = result * lax.dynamic_slice_in_dim(inverse, span * piece, piece, 1)
    return jnp.transpose(result, (1, 0, 2))


def solution(mesh):
    in_specs = (
        P("seg", ("groups", "chan"), None),
        P(("groups", "chan")),
        P(("groups", "chan")),
        P(),
    )
    out_specs = P(("groups", "chan", "seg"), None, "freq")
    return jax.shard_map(shards, mesh=mesh, in_specs=in_specs, out_specs=out_specs, check_vma=False)
```

```python
import functools
import math

import jax
import jax.numpy as jnp
import numpy as np
from jax import lax
from jax.experimental import pallas as pl
from jax.experimental.pallas import tpu as pltpu
from jax.sharding import PartitionSpec as P
import ml_dtypes

HALF = 32
LAGS = 512
F = 2048
TILE = 128
EPSILON = 1e-06
MIB = 1 << 20
GROUPS = (6, 9)


def tables(length, parts):
    bins_dev = F // parts
    tiles = bins_dev // TILE
    cosines = np.cos(np.arange(length) * (2.0 * math.pi / length))
    sines = -np.sin(np.arange(length) * (2.0 * math.pi / length))
    cos16 = cosines.astype(np.float32).astype(ml_dtypes.bfloat16)
    sin16 = sines.astype(np.float32).astype(ml_dtypes.bfloat16)
    samples = np.arange(length)[:, None]
    fourier = np.zeros((parts, tiles + 1, length, 2 * TILE), ml_dtypes.bfloat16)
    for part in range(parts):
        for tile in range(tiles + 1):
            first = part * bins_dev + (tile - 1) * TILE
            bin_index = first + np.arange(TILE)
            keep = np.ones((TILE,), bool)
            if tile == 0:
                lane = np.arange(TILE)
                after = part * bins_dev + bins_dev + lane
                before = part * bins_dev - TILE + lane
                bin_index = np.where(lane < HALF, after, before)
                keep = ((lane < HALF) & (after < F)) | ((lane >= TILE - HALF) & (before >= 0))
            phases = samples * bin_index[None, :] % length
            zero = ml_dtypes.bfloat16(0)
            fourier[part, tile, :, :TILE] = np.where(keep, cos16[phases], zero)
            fourier[part, tile, :, TILE:] = np.where(keep, sin16[phases], zero)
    lag_part = LAGS // parts
    delay = np.zeros((parts, 2 * bins_dev, LAGS), ml_dtypes.bfloat16)
    scaling = 1.0 / math.sqrt(F)
    for part in range(parts):
        shifts = np.roll(np.arange(LAGS), -part * lag_part) - LAGS // 2
        for tile in range(tiles):
            bin_index = part * bins_dev + tile * TILE + np.arange(TILE)
            phases = bin_index[:, None] * shifts[None, :] % length
            rows = tile * 2 * TILE
            delay[part, rows : rows + TILE] = (cosines[phases] * scaling).astype(ml_dtypes.bfloat16)
            delay[part, rows + TILE : rows + 2 * TILE] = (sines[phases] * scaling).astype(ml_dtypes.bfloat16)
    return fourier, delay


def whiten_kernel(plan, scalars, table_ref, *refs):
    (first, stop), _, tiles = plan
    refs = list(refs)
    x, limits = refs.pop(0), refs.pop(0)
    if first:
        carried_spectrum, carried_power = refs.pop(0), refs.pop(0)
    one_ref, two_ref = refs.pop(0), refs.pop(0)
    handed = stop <= tiles
    if handed:
        handed_spectrum, handed_power = refs.pop(0), refs.pop(0)
    spectra, power, band, eff = refs
    step = pl.program_id(0)
    made = stop - first
    segs, half, _ = one_ref.shape
    chans = 2 * half
    edge = 0 if first else 3
    lag = 1 if first else 3
    even = scalars[2] == 0

    def store():
        block = jnp.dot(x[...], table_ref[...], preferred_element_type=jnp.float32)
        slot = step + 1
        spectra[slot] = block
        re, im = block[:, :TILE], block[:, TILE:]
        power[slot + 2] = (re * re + im * im).astype(jnp.bfloat16)

    def finish():
        tile = first + step - 2
        slot = step - 1
        before, after = slot + 1, jnp.where(tile == tiles, edge, slot + 3)
        window = jnp.dot(power[before], band[:TILE], preferred_element_type=jnp.float32)
        window += jnp.dot(power[slot + 2], band[TILE : 2 * TILE], preferred_element_type=jnp.float32)
        window += jnp.dot(power[after], band[2 * TILE :], preferred_element_type=jnp.float32)
        bin_index = scalars[0] * (tiles * TILE) + (tile - 1) * TILE + lax.broadcasted_iota(jnp.int32, (1, TILE), 1)
        count = jnp.minimum(bin_index + HALF, F - 1) - jnp.maximum(bin_index - HALF, 0) + 1
        inverse = 1.0 / count.astype(jnp.float32)
        for seg in range(segs):
            row = seg * chans
            scale = lax.rsqrt(window[row : row + chans] * inverse + EPSILON)
            number = (scalars[1] + seg).astype(jnp.float32)
            scale = jnp.where(number < eff[...], scale, 0.0)
            for lanes in (slice(0, TILE), slice(TILE, 2 * TILE)):
                white = spectra[slot, row : row + chans, lanes] * scale
                lo, hi = white[:half], white[half:]
                one_ref[seg, :, lanes] = jnp.where(even, hi, lo).astype(jnp.bfloat16)
                two_ref[seg, :, lanes] = jnp.where(even, lo, hi).astype(jnp.bfloat16)

    @pl.when(step == 0)
    def _():
        row = lax.broadcasted_iota(jnp.int32, (3 * TILE, TILE), 0)
        column = lax.broadcasted_iota(jnp.int32, (3 * TILE, TILE), 1)
        near = jnp.abs(row - TILE - column) <= HALF
        band[...] = near.astype(jnp.float32).astype(jnp.bfloat16)
        eff[...] = jnp.transpose(jnp.broadcast_to(limits[...], (chans, chans)))
        if first:
            spectra[0] = carried_spectrum[...]
            power[0:3] = carried_power[...]

    @pl.when(step < lag)
    def _():
        store()

    @pl.when((step >= lag) & (step < made))
    def _():
        finish()
        store()

    @pl.when(step >= made)
    def _():
        finish()

    if handed:

        @pl.when(step == made)
        def _():
            handed_spectrum[...] = spectra[made]
            handed_power[0] = power[edge]
            handed_power[1] = power[made + 1]
            handed_power[2] = power[made + 2]


def whiten(plan, scalars, operands, fourier, segs, chans):
    (first, stop), (done_first, done_stop), tiles = plan
    made, done = stop - first, done_stop - done_first
    half, total, length = chans // 2, segs * chans, fourier.shape[2]
    lag = 1 if first else 3
    out = jax.ShapeDtypeStruct((segs, half, 2 * TILE * done), jnp.bfloat16)
    out_spec = pl.BlockSpec((segs, half, 2 * TILE), lambda j, p: (0, 0, jnp.clip(j - lag, 0, done - 1)))
    out_shape, out_specs = [out, out], [out_spec, out_spec]
    scratch = [
        pltpu.VMEM((made + 1, total, 2 * TILE), jnp.float32),
        pltpu.VMEM((made + 3, total, TILE), jnp.bfloat16),
        pltpu.VMEM((3 * TILE, TILE), jnp.bfloat16),
        pltpu.VMEM((chans, chans), jnp.float32),
    ]
    here = pl.BlockSpec(memory_space=pltpu.VMEM)
    if stop <= tiles:
        out_shape += [
            jax.ShapeDtypeStruct((total, 2 * TILE), jnp.float32),
            jax.ShapeDtypeStruct((3, total, TILE), jnp.bfloat16),
        ]
        out_specs += [here, here]
    return pl.pallas_call(
        functools.partial(whiten_kernel, plan),
        out_shape=out_shape,
        grid_spec=pltpu.PrefetchScalarGridSpec(
            num_scalar_prefetch=1,
            grid=(done + lag,),
            in_specs=[
                pl.BlockSpec(
                    (None, None, length, 2 * TILE), lambda j, p: (p[0], jnp.minimum(first + j, stop - 1), 0, 0)
                ),
            ]
            + [here] * len(operands),
            out_specs=out_specs,
            scratch_shapes=scratch,
        ),
        compiler_params=pltpu.CompilerParams(vmem_limit_bytes=36 * MIB),
        cost_estimate=pl.CostEstimate(
            flops=2 * total * length * 2 * TILE * made,
            bytes_accessed=2 * length * 2 * TILE * made + 2 * total * length,
            transcendentals=0,
        ),
        name="whiten",
    )(scalars, fourier, *operands)


def window_start(offset, chans):
    return jnp.minimum(chans // 2, chans - offset) // 16 * 16


def correlate_kernel(plan, scalars, one_ref, two_ref, got_one_ref, got_two_ref, delay_ref, *refs):
    tile_first, is_first, is_last = plan
    refs = list(refs)
    if is_first:
        own_counts, next_counts = refs.pop(0), refs.pop(0)
    else:
        sum_ref = refs.pop(0)
    if is_last:
        keep_ref, send_ref = refs.pop(0), refs.pop(0)
    else:
        total = refs.pop(0)
    if is_first:
        inverse_ref = refs.pop(0)
    if is_last:
        total = refs.pop(0)
    select, frame, far, cross = refs
    step, last = pl.program_id(0), pl.num_programs(0) - 1
    segs, half, _ = one_ref.shape
    chans = 2 * half
    slots = cross.shape[0] // chans
    even, known = scalars[1] == 0, scalars[2]

    @pl.when(step == 0)
    def _():
        total[...] = jnp.zeros_like(total) if is_first else sum_ref[...]
        row = lax.broadcasted_iota(jnp.int32, (chans, 2 * chans), 0)
        column = lax.broadcasted_iota(jnp.int32, (chans, 2 * chans), 1)
        for slot in range(slots):
            offset = scalars[3 + slot]
            match = (column == row + window_start(offset, chans) + offset) & (column < known)
            select[slot * chans : (slot + 1) * chans] = match.astype(jnp.float32).astype(jnp.bfloat16)
        if is_first:
            row = lax.broadcasted_iota(jnp.int32, (chans, chans), 0)
            column = lax.broadcasted_iota(jnp.int32, (chans, chans), 1)
            own, following = own_counts[...].astype(jnp.float32), next_counts[...].astype(jnp.float32)
            mine = jnp.sum(jnp.where(row == column, own, 0.0), axis=1, keepdims=True)
            for slot in range(slots):
                target = row + scalars[3 + slot]
                partner = jnp.where(column == target, own, 0.0) + jnp.where(column + chans == target, following, 0.0)
                partner = jnp.sum(partner, axis=1, keepdims=True)
                divisor = jnp.maximum(jnp.minimum(mine, partner), 1.0)
                inverse_ref[slot] = jnp.broadcast_to(1.0 / divisor, inverse_ref.shape[1:])

    order = ((one_ref, 2, 1), (two_ref, 1, 2), (got_one_ref, 3, 0), (got_two_ref, 0, 3))
    for ref, if_even, if_odd in order:
        spot = pl.ds(pl.multiple_of(jnp.where(even, if_even * half, if_odd * half), half), half)
        for seg in range(segs):
            frame[seg, spot, :] = ref[seg]
    for seg in range(segs):
        far[seg] = jnp.dot(select[...], frame[seg], preferred_element_type=jnp.float32)
    for slot in range(slots):
        start = window_start(scalars[3 + slot], chans)

        def rows(index, carry, slot=slot, start=start):
            real = jnp.zeros((16, TILE), jnp.float32)
            imag = jnp.zeros((16, TILE), jnp.float32)
            base = pl.multiple_of(start + index * 16, 16)
            spot = pl.multiple_of(slot * chans + index * 16, 16)
            for seg in range(segs):
                own = frame[seg, pl.ds(base, 16), :].astype(jnp.float32)
                own_re, own_im = own[:, :TILE], own[:, TILE:]
                far_re, far_im = far[seg, pl.ds(spot, 16), :TILE], far[seg, pl.ds(spot, 16), TILE:]
                real += own_re * far_re + own_im * far_im
                imag += own_im * far_re - own_re * far_im
            cross[pl.ds(spot, 16), :TILE] = real.astype(jnp.bfloat16)
            cross[pl.ds(spot, 16), TILE:] = imag.astype(jnp.bfloat16)
            return carry

        lax.fori_loop(0, chans // 16, rows, 0, unroll=True)
    total[...] += jnp.dot(cross[...], delay_ref[...], preferred_element_type=jnp.float32)

    if is_last:

        @pl.when(step == last)
        def _():
            keep = keep_ref.shape[2]
            keep_ref[...] = jnp.zeros_like(keep_ref)
            send_ref[...] = jnp.zeros_like(send_ref)
            for slot in range(slots):
                start = pl.multiple_of(window_start(scalars[3 + slot], chans), 16)
                block = total[slot * chans : (slot + 1) * chans]
                keep_ref[slot, pl.ds(start, chans), :] = block[:, :keep]
                send_ref[slot, pl.ds(start, chans), :] = block[:, keep:].astype(send_ref.dtype)


def correlate(plan, scalars, one, two, got_one, got_two, delay, extra, parts):
    tile_first, is_first, is_last = plan
    segs, half, columns = one.shape
    chans = 2 * half
    tiles = columns // (2 * TILE)
    slots = scalars.shape[0] - 3
    lags = delay.shape[2]
    keep = lags // parts
    spec = pl.BlockSpec((segs, half, 2 * TILE), lambda j, s: (0, 0, j))
    flat = pl.BlockSpec(memory_space=pltpu.VMEM)
    vector = pl.BlockSpec((1, chans), lambda j, s: (0, 0))
    frame = lambda width: pl.BlockSpec((slots, 3 * half, width), lambda j, s: (0, 0, 0))
    scratch = [
        pltpu.VMEM((slots * chans, 2 * chans), jnp.bfloat16),
        pltpu.VMEM((segs, 2 * chans, 2 * TILE), jnp.bfloat16),
        pltpu.VMEM((segs, slots * chans, 2 * TILE), jnp.float32),
        pltpu.VMEM((slots * chans, 2 * TILE), jnp.bfloat16),
    ]
    out_shape, out_specs = [], []
    if is_last:
        out_shape += [
            jax.ShapeDtypeStruct((slots, 3 * half, keep), jnp.float32),
            jax.ShapeDtypeStruct((slots, 3 * half, lags - keep), jnp.bfloat16),
        ]
        out_specs += [frame(keep), frame(lags - keep)]
        scratch = [pltpu.VMEM((slots * chans, lags), jnp.float32)] + scratch
    else:
        out_shape += [jax.ShapeDtypeStruct((slots * chans, lags), jnp.float32)]
        out_specs += [flat]
    if is_first:
        out_shape += [jax.ShapeDtypeStruct((slots, chans, keep), jnp.float32)]
        out_specs += [flat]
    return pl.pallas_call(
        functools.partial(correlate_kernel, plan),
        out_shape=out_shape,
        grid_spec=pltpu.PrefetchScalarGridSpec(
            num_scalar_prefetch=1,
            grid=(tiles,),
            in_specs=[spec, spec, spec, spec]
            + [pl.BlockSpec((None, 2 * TILE, lags), lambda j, s: (s[0], tile_first + j, 0))]
            + ([vector, vector] if is_first else [flat]),
            out_specs=out_specs,
            scratch_shapes=scratch,
        ),
        compiler_params=pltpu.CompilerParams(vmem_limit_bytes=32 * MIB),
        cost_estimate=pl.CostEstimate(
            flops=tiles * 2 * slots * chans * 2 * TILE * (segs * 2 * chans + lags),
            bytes_accessed=tiles * (4 * segs * half * 2 * TILE * 2),
            transcendentals=0,
        ),
        name="correlate",
    )(scalars, one, two, got_one, got_two, delay, *extra)


def swap(block, first):
    blocks, parts = lax.axis_size("chan"), lax.axis_size("freq")
    route = []
    for i in range(blocks):
        partner = i + 1 if (i - first) % 2 == 0 else i - 1
        alone = not 0 <= partner < blocks
        for part in range(parts):
            target = i * parts + (part + 1) % parts if alone else partner * parts + part
            route.append((i * parts + part, target))
    return lax.ppermute(block, ("chan", "freq"), route)


def returns(blocks, parts):
    near, far = {}, {}
    last = blocks - 1
    for i in range(blocks):
        near[i, 1] = (i - 1, 1) if i else (0, 0)
        near[i, 0] = (i + 1, 0) if i < last else (last, 1)
        far[i, 0] = (i - 1, 1) if i else (0, 0)
        far[i, 1] = (i + 1, 0) if i < last else (last, 1)
    routes = []
    for steps in (near, far):
        route = []
        for source, target in steps.items():
            for part in range(parts):
                end = (part + 1) % parts if source == target else part
                route.append(((2 * source[0] + source[1]) * parts + part, (2 * target[0] + target[1]) * parts + end))
        routes.append(route)
    return routes


def reduced(span, keep, chans, has_next):
    spans, blocks = lax.axis_size("seg"), lax.axis_size("chan")
    half = chans // 2
    back = lax.ppermute(keep[:, :half].astype(jnp.bfloat16), "chan", [(i, (i - 1) % blocks) for i in range(blocks)])
    back = jnp.where(has_next, back.astype(jnp.float32), 0.0)
    keep = keep[:, half:] + jnp.pad(back, ((0, 0), (chans - half, 0), (0, 0)))
    piece = chans // spans
    result = lax.dynamic_slice_in_dim(keep, span * piece, piece, 1)
    for step in range(1, spans):
        target = lax.rem(span + step, spans)
        block = lax.dynamic_slice_in_dim(keep, target * piece, piece, 1).astype(jnp.bfloat16)
        block = lax.ppermute(block, "seg", [(i, (i + step) % spans) for i in range(spans)])
        result = result + block.astype(jnp.float32)
    return result


def shards(traces, dead_mask, seg_counts, offsets):
    segs, chans, length = traces.shape
    half = chans // 2
    parts, spans, blocks = lax.axis_size("freq"), lax.axis_size("seg"), lax.axis_size("chan")
    assert parts == 2
    fourier, delay = (jnp.asarray(table) for table in tables(length, parts))
    tiles = fourier.shape[1] - 1
    part = lax.axis_index("freq").astype(jnp.int32)
    span = lax.axis_index("seg").astype(jnp.int32)
    place = lax.axis_index("chan").astype(jnp.int32)
    has_next = place < blocks - 1
    counts = seg_counts.reshape(1, chans)
    limits = jnp.where(dead_mask > 0, seg_counts, 0).astype(jnp.float32).reshape(1, chans)
    next_counts = lax.ppermute(seg_counts, "chan", [(i, (i - 1) % blocks) for i in range(blocks)]).reshape(1, chans)
    parity = place & 1
    scalars = jnp.stack([part, span * segs, parity])
    known = jnp.where(has_next, 4 * half, 3 * half)
    settings = jnp.concatenate([jnp.stack([part, parity, known]), offsets])

    groups, operands, made = [], [traces.reshape(segs * chans, length), limits], 0
    for stop in GROUPS:
        plan = ((made, stop), (max(made - 1, 1), stop - 1 if stop <= tiles else tiles + 1), tiles)
        one, two, *passed = whiten(plan, scalars, operands, fourier, segs, chans)
        operands = operands[:2] + passed
        if groups:
            send_one, send_two = one, two
        else:
            send_one, send_two, next_counts = lax.optimization_barrier((one, two, next_counts))
        got_one, got_two = swap(send_one, 0), swap(send_two, 1)
        groups.append((one, two, got_one, got_two))
        made = stop
    extra, tile_first = [counts, next_counts], 0
    for index, group in enumerate(groups):
        plan = (tile_first, index == 0, index == len(groups) - 1)
        results = list(correlate(plan, settings, *group, delay, extra, parts))
        if index == 0:
            inverse = results.pop()
        extra = results
        tile_first += group[0].shape[2] // (2 * TILE)
    keep, send = results
    keep = keep + lax.ppermute(send, "freq", [(0, 1), (1, 0)]).astype(jnp.float32)
    if spans == 2:
        lower, upper = keep[:, half:chans], keep[:, chans:]
        mine = jnp.where(span == 0, lower, upper)
        other = jnp.where(span == 0, upper, lower).astype(jnp.bfloat16)
        back = keep[:, :half].astype(jnp.bfloat16)
        other = lax.ppermute(other, "seg", [(0, 1), (1, 0)])
        route_near, route_far = returns(blocks, parts)
        near = lax.ppermute(back, ("chan", "seg", "freq"), route_near)
        far = lax.ppermute(back, ("chan", "seg", "freq"), route_far)
        returned = jnp.where(has_next & (span == 1), near.astype(jnp.float32) + far.astype(jnp.float32), 0.0)
        result = mine + other.astype(jnp.float32) + returned
        result = result * jnp.where(span == 0, inverse[:, :half], inverse[:, half:])
    else:
        piece = chans // spans
        result = reduced(span, keep, chans, has_next)
        result = result * lax.dynamic_slice_in_dim(inverse, span * piece, piece, 1)
    return jnp.transpose(result, (1, 0, 2))


def solution(mesh):
    in_specs = (
        P("seg", ("groups", "chan"), None),
        P(("groups", "chan")),
        P(("groups", "chan")),
        P(),
    )
    out_specs = P(("groups", "chan", "seg"), None, "freq")
    return jax.shard_map(shards, mesh=mesh, in_specs=in_specs, out_specs=out_specs, check_vma=False)
```

```python
import functools
import math

import jax
import jax.numpy as jnp
import numpy as np
from jax import lax
from jax.experimental import pallas as pl
from jax.experimental.pallas import tpu as pltpu
from jax.sharding import PartitionSpec as P
import ml_dtypes

HALF = 32
LAGS = 512
F = 2048
TILE = 128
EPSILON = 1e-06
MIB = 1 << 20
GROUPS = (5, 8, 9)


def tables(length, parts):
    bins_dev = F // parts
    tiles = bins_dev // TILE
    cosines = np.cos(np.arange(length) * (2.0 * math.pi / length))
    sines = -np.sin(np.arange(length) * (2.0 * math.pi / length))
    cos16 = cosines.astype(np.float32).astype(ml_dtypes.bfloat16)
    sin16 = sines.astype(np.float32).astype(ml_dtypes.bfloat16)
    samples = np.arange(length)[:, None]
    fourier = np.zeros((parts, tiles + 2, length, 2 * TILE), ml_dtypes.bfloat16)
    for part in range(parts):
        for tile in range(tiles + 1):
            first = part * bins_dev + (tile - 1) * TILE
            bin_index = first + np.arange(TILE)
            keep = np.ones((TILE,), bool)
            if tile == 0:
                lane = np.arange(TILE)
                after = part * bins_dev + bins_dev + lane
                before = part * bins_dev - TILE + lane
                bin_index = np.where(lane < HALF, after, before)
                keep = ((lane < HALF) & (after < F)) | ((lane >= TILE - HALF) & (before >= 0))
            phases = samples * bin_index[None, :] % length
            zero = ml_dtypes.bfloat16(0)
            fourier[part, tile, :, :TILE] = np.where(keep, cos16[phases], zero)
            fourier[part, tile, :, TILE:] = np.where(keep, sin16[phases], zero)
    lag_part = LAGS // parts
    delay = np.zeros((2 * bins_dev, LAGS), ml_dtypes.bfloat16)
    scaling = 1.0 / math.sqrt(F)
    for part in range(parts):
        shifts = np.roll(np.arange(LAGS), -part * lag_part) - LAGS // 2
        for tile in range(tiles):
            bin_index = part * bins_dev + tile * TILE + np.arange(TILE)
            phases = bin_index[:, None] * shifts[None, :] % length
            rows = tile * 2 * TILE
            delay[rows : rows + TILE] = (cosines[phases] * scaling).astype(ml_dtypes.bfloat16)
            delay[rows + TILE : rows + 2 * TILE] = (sines[phases] * scaling).astype(ml_dtypes.bfloat16)
        blocks = delay.reshape(tiles, 2 * TILE, parts, lag_part).transpose(2, 0, 1, 3)
        fourier[part, tiles + 1, : tiles * parts * 2 * TILE, :lag_part] = blocks.reshape(-1, lag_part)
    return fourier


def whiten_kernel(plan, scalars, table_ref, *refs):
    (first, stop), _, tiles = plan
    refs = list(refs)
    x, limits = refs.pop(0), refs.pop(0)
    if first:
        carried_spectrum, carried_power = refs.pop(0), refs.pop(0)
    one_ref, two_ref = refs.pop(0), refs.pop(0)
    handed = stop <= tiles
    if handed:
        handed_spectrum, handed_power = refs.pop(0), refs.pop(0)
    spectra, power, band, eff = refs
    step = pl.program_id(0)
    made = stop - first
    segs, half, _ = one_ref.shape
    chans = 2 * half
    edge = 0 if first else 3
    lag = 1 if first else 3
    even = scalars[2] == 0

    def store():
        block = jnp.dot(x[...], table_ref[...], preferred_element_type=jnp.float32)
        slot = step + 1
        spectra[slot] = block
        re, im = block[:, :TILE], block[:, TILE:]
        power[slot + 2] = (re * re + im * im).astype(jnp.bfloat16)

    def finish():
        tile = first + step - 2
        slot = step - 1
        before, after = slot + 1, jnp.where(tile == tiles, edge, slot + 3)
        window = jnp.dot(power[before], band[:TILE], preferred_element_type=jnp.float32)
        window += jnp.dot(power[slot + 2], band[TILE : 2 * TILE], preferred_element_type=jnp.float32)
        window += jnp.dot(power[after], band[2 * TILE :], preferred_element_type=jnp.float32)
        bin_index = scalars[0] * (tiles * TILE) + (tile - 1) * TILE + lax.broadcasted_iota(jnp.int32, (1, TILE), 1)
        count = jnp.minimum(bin_index + HALF, F - 1) - jnp.maximum(bin_index - HALF, 0) + 1
        inverse = 1.0 / count.astype(jnp.float32)
        for seg in range(segs):
            row = seg * chans
            scale = lax.rsqrt(window[row : row + chans] * inverse + EPSILON)
            number = (scalars[1] + seg).astype(jnp.float32)
            scale = jnp.where(number < eff[...], scale, 0.0)
            for lanes in (slice(0, TILE), slice(TILE, 2 * TILE)):
                white = spectra[slot, row : row + chans, lanes] * scale
                lo, hi = white[:half], white[half:]
                one_ref[seg, :, lanes] = jnp.where(even, hi, lo).astype(jnp.bfloat16)
                two_ref[seg, :, lanes] = jnp.where(even, lo, hi).astype(jnp.bfloat16)

    @pl.when(step == 0)
    def _():
        row = lax.broadcasted_iota(jnp.int32, (3 * TILE, TILE), 0)
        column = lax.broadcasted_iota(jnp.int32, (3 * TILE, TILE), 1)
        near = jnp.abs(row - TILE - column) <= HALF
        band[...] = near.astype(jnp.float32).astype(jnp.bfloat16)
        eff[...] = jnp.transpose(jnp.broadcast_to(limits[...], (chans, chans)))
        if first:
            spectra[0] = carried_spectrum[...]
            power[0:3] = carried_power[...]

    @pl.when(step < lag)
    def _():
        store()

    @pl.when((step >= lag) & (step < made))
    def _():
        finish()
        store()

    @pl.when(step >= made)
    def _():
        finish()

    if handed:

        @pl.when(step == made)
        def _():
            handed_spectrum[...] = spectra[made]
            handed_power[0] = power[edge]
            handed_power[1] = power[made + 1]
            handed_power[2] = power[made + 2]


def whiten(plan, scalars, operands, fourier, segs, chans):
    (first, stop), (done_first, done_stop), tiles = plan
    made, done = stop - first, done_stop - done_first
    half, total, length = chans // 2, segs * chans, fourier.shape[2]
    lag = 1 if first else 3
    out = jax.ShapeDtypeStruct((segs, half, 2 * TILE * done), jnp.bfloat16)
    out_spec = pl.BlockSpec((segs, half, 2 * TILE), lambda j, p: (0, 0, jnp.clip(j - lag, 0, done - 1)))
    out_shape, out_specs = [out, out], [out_spec, out_spec]
    scratch = [
        pltpu.VMEM((made + 1, total, 2 * TILE), jnp.float32),
        pltpu.VMEM((made + 3, total, TILE), jnp.bfloat16),
        pltpu.VMEM((3 * TILE, TILE), jnp.bfloat16),
        pltpu.VMEM((chans, chans), jnp.float32),
    ]
    here = pl.BlockSpec(memory_space=pltpu.VMEM)
    if stop <= tiles:
        out_shape += [
            jax.ShapeDtypeStruct((total, 2 * TILE), jnp.float32),
            jax.ShapeDtypeStruct((3, total, TILE), jnp.bfloat16),
        ]
        out_specs += [here, here]
    return pl.pallas_call(
        functools.partial(whiten_kernel, plan),
        out_shape=out_shape,
        grid_spec=pltpu.PrefetchScalarGridSpec(
            num_scalar_prefetch=1,
            grid=(done + lag,),
            in_specs=[
                pl.BlockSpec(
                    (None, None, length, 2 * TILE), lambda j, p: (p[0], jnp.minimum(first + j, stop - 1), 0, 0)
                ),
            ]
            + [here] * len(operands),
            out_specs=out_specs,
            scratch_shapes=scratch,
        ),
        compiler_params=pltpu.CompilerParams(vmem_limit_bytes=24 * MIB),
        cost_estimate=pl.CostEstimate(
            flops=2 * total * length * 2 * TILE * made,
            bytes_accessed=2 * length * 2 * TILE * made + 2 * total * length,
            transcendentals=0,
        ),
        name="whiten",
    )(scalars, fourier, *operands)


def window_start(offset, chans):
    return jnp.minimum(chans // 2, chans - offset) // 16 * 16


def correlate_kernel(plan, scalars, one_ref, two_ref, got_one_ref, got_two_ref, table_hbm, *refs):
    tile_first, is_first, is_last = plan
    refs = list(refs)
    if is_first:
        own_counts, next_counts = refs.pop(0), refs.pop(0)
    else:
        sum_ref = refs.pop(0)
    if is_last:
        keep_ref, send_ref = refs.pop(0), refs.pop(0)
    else:
        total_ref = refs.pop(0)
    if is_first:
        inverse_ref = refs.pop(0)
    select, frame, far, cross, delay, sems = refs
    segs, half, columns = one_ref.shape
    tiles = columns // (2 * TILE)
    chans = 2 * half
    slots = cross.shape[0] // chans
    parts, depth, width = delay.shape
    place, length = table_hbm.shape[1] - 1, table_hbm.shape[2] // parts
    even, known = scalars[1] == 0, scalars[2]

    copies = []
    for part in range(parts):
        rows = pl.ds(part * length + tile_first * 2 * TILE, depth)
        source = table_hbm.at[scalars[0], place, rows, :]
        copies.append(pltpu.make_async_copy(source, delay.at[part], sems.at[part]))
        copies[part].start()

    row = lax.broadcasted_iota(jnp.int32, (chans, 2 * chans), 0)
    column = lax.broadcasted_iota(jnp.int32, (chans, 2 * chans), 1)
    for slot in range(slots):
        offset = scalars[3 + slot]
        match = (column == row + window_start(offset, chans) + offset) & (column < known)
        select[slot * chans : (slot + 1) * chans] = match.astype(jnp.float32).astype(jnp.bfloat16)

    order = ((one_ref, 2, 1), (two_ref, 1, 2), (got_one_ref, 3, 0), (got_two_ref, 0, 3))
    for tile in range(tiles):
        for ref, if_even, if_odd in order:
            spot = pl.ds(pl.multiple_of(jnp.where(even, if_even * half, if_odd * half), half), half)
            for seg in range(segs):
                frame[tile, seg, spot, :] = ref[seg, :, tile * 2 * TILE : (tile + 1) * 2 * TILE]
        for seg in range(segs):
            far[tile, seg] = jnp.dot(select[...], frame[tile, seg], preferred_element_type=jnp.float32)
        for slot in range(slots):
            start = window_start(scalars[3 + slot], chans)
            for index in range(chans // 16):
                real = jnp.zeros((16, TILE), jnp.float32)
                imag = jnp.zeros((16, TILE), jnp.float32)
                base = pl.multiple_of(start + index * 16, 16)
                spot = slice(slot * chans + index * 16, slot * chans + index * 16 + 16)
                for seg in range(segs):
                    own = frame[tile, seg, pl.ds(base, 16), :].astype(jnp.float32)
                    own_re, own_im = own[:, :TILE], own[:, TILE:]
                    far_re, far_im = far[tile, seg, spot, :TILE], far[tile, seg, spot, TILE:]
                    real += own_re * far_re + own_im * far_im
                    imag += own_im * far_re - own_re * far_im
                lane = tile * 2 * TILE
                cross[spot, lane : lane + TILE] = real.astype(jnp.bfloat16)
                cross[spot, lane + TILE : lane + 2 * TILE] = imag.astype(jnp.bfloat16)

    if is_first:
        row = lax.broadcasted_iota(jnp.int32, (chans, chans), 0)
        column = lax.broadcasted_iota(jnp.int32, (chans, chans), 1)
        own, following = own_counts[...].astype(jnp.float32), next_counts[...].astype(jnp.float32)
        mine = jnp.sum(jnp.where(row == column, own, 0.0), axis=1, keepdims=True)
        for slot in range(slots):
            target = row + scalars[3 + slot]
            partner = jnp.where(column == target, own, 0.0) + jnp.where(column + chans == target, following, 0.0)
            partner = jnp.sum(partner, axis=1, keepdims=True)
            divisor = jnp.maximum(jnp.minimum(mine, partner), 1.0)
            inverse_ref[slot] = jnp.broadcast_to(1.0 / divisor, inverse_ref.shape[1:])
    if is_last:
        keep_ref[...] = jnp.zeros_like(keep_ref)
        send_ref[...] = jnp.zeros_like(send_ref)

    for part in range(parts):
        copies[part].wait()
        lanes = slice(part * width, (part + 1) * width)
        for slot in range(slots):
            spot = slice(slot * chans, (slot + 1) * chans)
            term = jnp.dot(cross[spot], delay[part], preferred_element_type=jnp.float32)
            if not is_first:
                term += sum_ref[spot, lanes]
            if not is_last:
                total_ref[spot, lanes] = term
                continue
            rows = pl.ds(pl.multiple_of(window_start(scalars[3 + slot], chans), 16), chans)
            if part == 0:
                keep_ref[slot, rows, :] = term
            else:
                send_ref[slot, rows, lanes.start - width : lanes.stop - width] = term.astype(send_ref.dtype)


def correlate(plan, scalars, one, two, got_one, got_two, table, extra):
    tile_first, is_first, is_last = plan
    segs, half, columns = one.shape
    chans = 2 * half
    tiles = columns // (2 * TILE)
    slots = scalars.shape[0] - 3
    parts, keep = table.shape[0], table.shape[3]
    lags = parts * keep
    here = pl.BlockSpec(memory_space=pltpu.VMEM)
    if is_last:
        out_shape = [
            jax.ShapeDtypeStruct((slots, 3 * half, keep), jnp.float32),
            jax.ShapeDtypeStruct((slots, 3 * half, lags - keep), jnp.bfloat16),
        ]
    else:
        out_shape = [jax.ShapeDtypeStruct((slots * chans, lags), jnp.float32)]
    if is_first:
        out_shape += [jax.ShapeDtypeStruct((slots, chans, keep), jnp.float32)]
    return pl.pallas_call(
        functools.partial(correlate_kernel, plan),
        out_shape=out_shape,
        grid_spec=pltpu.PrefetchScalarGridSpec(
            num_scalar_prefetch=1,
            grid=(),
            in_specs=[here] * 4 + [pl.BlockSpec(memory_space=pl.ANY)] + [here] * len(extra),
            out_specs=[here] * len(out_shape),
            scratch_shapes=[
                pltpu.VMEM((slots * chans, 2 * chans), jnp.bfloat16),
                pltpu.VMEM((tiles, segs, 2 * chans, 2 * TILE), jnp.bfloat16),
                pltpu.VMEM((tiles, segs, slots * chans, 2 * TILE), jnp.float32),
                pltpu.VMEM((slots * chans, columns), jnp.bfloat16),
                pltpu.VMEM((parts, columns, keep), jnp.bfloat16),
                pltpu.SemaphoreType.DMA((parts,)),
            ],
        ),
        compiler_params=pltpu.CompilerParams(vmem_limit_bytes=28 * MIB),
        cost_estimate=pl.CostEstimate(
            flops=tiles * 2 * slots * chans * 2 * TILE * (segs * 2 * chans + lags),
            bytes_accessed=tiles * (4 * segs * half * 2 * TILE * 2),
            transcendentals=0,
        ),
        name="correlate",
    )(scalars, one, two, got_one, got_two, table, *extra)


def swap(block, first):
    blocks, parts = lax.axis_size("chan"), lax.axis_size("freq")
    route = []
    for i in range(blocks):
        partner = i + 1 if (i - first) % 2 == 0 else i - 1
        alone = not 0 <= partner < blocks
        for part in range(parts):
            target = i * parts + (part + 1) % parts if alone else partner * parts + part
            route.append((i * parts + part, target))
    return lax.ppermute(block, ("chan", "freq"), route)


def returns(blocks, parts):
    near, far = {}, {}
    last = blocks - 1
    for i in range(blocks):
        near[i, 1] = (i - 1, 1) if i else (0, 0)
        near[i, 0] = (i + 1, 0) if i < last else (last, 1)
        far[i, 0] = (i - 1, 1) if i else (0, 0)
        far[i, 1] = (i + 1, 0) if i < last else (last, 1)
    routes = []
    for steps in (near, far):
        route = []
        for source, target in steps.items():
            for part in range(parts):
                end = (part + 1) % parts if source == target else part
                route.append(((2 * source[0] + source[1]) * parts + part, (2 * target[0] + target[1]) * parts + end))
        routes.append(route)
    return routes


def reduced(span, keep, chans, has_next):
    spans, blocks = lax.axis_size("seg"), lax.axis_size("chan")
    half = chans // 2
    back = lax.ppermute(keep[:, :half].astype(jnp.bfloat16), "chan", [(i, (i - 1) % blocks) for i in range(blocks)])
    back = jnp.where(has_next, back.astype(jnp.float32), 0.0)
    keep = keep[:, half:] + jnp.pad(back, ((0, 0), (chans - half, 0), (0, 0)))
    piece = chans // spans
    result = lax.dynamic_slice_in_dim(keep, span * piece, piece, 1)
    for step in range(1, spans):
        target = lax.rem(span + step, spans)
        block = lax.dynamic_slice_in_dim(keep, target * piece, piece, 1).astype(jnp.bfloat16)
        block = lax.ppermute(block, "seg", [(i, (i + step) % spans) for i in range(spans)])
        result = result + block.astype(jnp.float32)
    return result


def shards(traces, dead_mask, seg_counts, offsets):
    segs, chans, length = traces.shape
    half = chans // 2
    parts, spans, blocks = lax.axis_size("freq"), lax.axis_size("seg"), lax.axis_size("chan")
    assert parts == 2
    table = jnp.asarray(tables(length, parts))
    tiles = table.shape[1] - 2
    part = lax.axis_index("freq").astype(jnp.int32)
    span = lax.axis_index("seg").astype(jnp.int32)
    place = lax.axis_index("chan").astype(jnp.int32)
    has_next = place < blocks - 1
    counts = seg_counts.reshape(1, chans)
    limits = jnp.where(dead_mask > 0, seg_counts, 0).astype(jnp.float32).reshape(1, chans)
    parity = place & 1
    next_counts = swap(seg_counts, 0), swap(seg_counts, 1)
    scalars = jnp.stack([part, span * segs, parity])
    known = jnp.where(has_next, 4 * half, 3 * half)
    settings = jnp.concatenate([jnp.stack([part, parity, known]), offsets])

    groups, operands, made = [], [traces.reshape(segs * chans, length), limits], 0
    for stop in GROUPS:
        plan = ((made, stop), (max(made - 1, 1), stop - 1 if stop <= tiles else tiles + 1), tiles)
        one, two, *passed = whiten(plan, scalars, operands, table, segs, chans)
        operands = operands[:2] + passed
        if groups:
            send_one, send_two = one, two
        else:
            send_one, send_two, next_counts = lax.optimization_barrier((one, two, next_counts))
            next_counts = jnp.where(parity == 0, *next_counts).reshape(1, chans)
        got_one, got_two = swap(send_one, 0), swap(send_two, 1)
        groups.append((one, two, got_one, got_two))
        made = stop
    extra, tile_first = [counts, next_counts], 0
    for index, group in enumerate(groups):
        plan = (tile_first, index == 0, index == len(groups) - 1)
        results = list(correlate(plan, settings, *group, table, extra))
        if index == 0:
            inverse = results.pop()
        extra = results
        tile_first += group[0].shape[2] // (2 * TILE)
    keep, send = results
    keep = keep + lax.ppermute(send, "freq", [(0, 1), (1, 0)]).astype(jnp.float32)
    if spans == 2:
        lower, upper = keep[:, half:chans], keep[:, chans:]
        mine = jnp.where(span == 0, lower, upper)
        other = jnp.where(span == 0, upper, lower).astype(jnp.bfloat16)
        back = keep[:, :half].astype(jnp.bfloat16)
        other = lax.ppermute(other, "seg", [(0, 1), (1, 0)])
        route_near, route_far = returns(blocks, parts)
        near = lax.ppermute(back, ("chan", "seg", "freq"), route_near)
        far = lax.ppermute(back, ("chan", "seg", "freq"), route_far)
        returned = jnp.where(has_next & (span == 1), near.astype(jnp.float32) + far.astype(jnp.float32), 0.0)
        result = mine + other.astype(jnp.float32) + returned
        result = result * jnp.where(span == 0, inverse[:, :half], inverse[:, half:])
    else:
        piece = chans // spans
        result = reduced(span, keep, chans, has_next)
        result = result * lax.dynamic_slice_in_dim(inverse, span * piece, piece, 1)
    return jnp.transpose(result, (1, 0, 2))


def solution(mesh):
    in_specs = (
        P("seg", ("groups", "chan"), None),
        P(("groups", "chan")),
        P(("groups", "chan")),
        P(),
    )
    out_specs = P(("groups", "chan", "seg"), None, "freq")
    return jax.shard_map(shards, mesh=mesh, in_specs=in_specs, out_specs=out_specs, check_vma=False)
```

```python
import functools
import math

import jax
import jax.numpy as jnp
import numpy as np
from jax import lax
from jax.experimental import pallas as pl
from jax.experimental.pallas import tpu as pltpu
from jax.sharding import PartitionSpec as P
import ml_dtypes

HALF = 32
LAGS = 512
F = 2048
TILE = 128
EPSILON = 1e-06
MIB = 1 << 20
EXTRA = 16
LAG_TILES = 4
GROUPS = (4, 7, 9)
AHEAD = (5, 8, 9)


def tables(length, parts):
    bins_dev = F // parts
    tiles = bins_dev // TILE
    cosines = np.cos(np.arange(length) * (2.0 * math.pi / length))
    sines = -np.sin(np.arange(length) * (2.0 * math.pi / length))
    cos16 = cosines.astype(np.float32).astype(ml_dtypes.bfloat16)
    sin16 = sines.astype(np.float32).astype(ml_dtypes.bfloat16)
    samples = np.arange(length)[:, None]
    fourier = np.zeros((parts, tiles + 2, length, 2 * TILE), ml_dtypes.bfloat16)
    lag_part = LAGS // parts
    delay = np.zeros((2 * bins_dev, LAGS), ml_dtypes.bfloat16)
    scaling = 1.0 / math.sqrt(F)
    for part in range(parts):
        shifts = np.roll(np.arange(LAGS), -part * lag_part) - LAGS // 2
        for tile in range(tiles + 1):
            place = tile * TILE + np.arange(TILE)
            bin_index = F - 1 - place if part else place
            phases = samples * bin_index[None, :] % length
            width = TILE if tile < tiles else HALF
            fourier[part, tile, :, :width] = cos16[phases[:, :width]]
            fourier[part, tile, :, TILE : TILE + width] = sin16[phases[:, :width]]
            if tile < tiles:
                phases = bin_index[:, None] * shifts[None, :] % length
                rows = tile * 2 * TILE
                delay[rows : rows + TILE] = (cosines[phases] * scaling).astype(ml_dtypes.bfloat16)
                delay[rows + TILE : rows + 2 * TILE] = (sines[phases] * scaling).astype(ml_dtypes.bfloat16)
        blocks = delay.reshape(tiles, 2 * TILE, parts, lag_part).transpose(2, 0, 1, 3)
        fourier[part, tiles + 1, : tiles * parts * 2 * TILE, :lag_part] = blocks.reshape(-1, lag_part)
    return fourier


def whiten_kernel(plan, names, *refs):
    first, stop, further, tiles = plan
    refs = dict(zip(names, refs))
    x, counts, table_hbm = refs["x"], refs["counts"], refs["table"]
    one_ref, two_ref, eff, band, sems = (refs[name] for name in ("one", "two", "eff", "band", "sems"))
    chans = eff.shape[0]
    total, length = x.shape
    segs, half = total // chans, chans // 2
    even = lax.axis_index("chan") & 1 == 0
    buffers, had = refs.get("buffers"), first + (refs["table_in"].shape[0] if first else 0)

    def fetch(tile):
        source = table_hbm.at[lax.axis_index("freq"), tile]
        target = refs["table_out"].at[tile - stop] if tile >= stop else buffers.at[tile - had]
        return pltpu.make_async_copy(source, target, sems.at[tile - first])

    def table_of(tile):
        return refs["table_in"].at[tile - first] if tile < had else buffers.at[tile - had]

    def spectrum_of(tile):
        if tile < first:
            return refs["spectrum_in"]
        return refs["spectrum_out"] if tile == stop - 1 <= tiles - 1 else refs["spectra"].at[tile - first]

    def power_of(tile):
        if tile < first:
            return refs["power_in"].at[tile - first + 2]
        return refs["power_out"].at[tile - stop + 2] if stop - 2 <= tile and stop <= tiles else refs["power"].at[tile - first]

    def store(tile):
        block = jnp.dot(x[...], table_of(tile)[...], preferred_element_type=jnp.float32)
        spectrum_of(tile)[...] = block
        re, im = block[:, :TILE], block[:, TILE:]
        power_of(tile)[...] = (re * re + im * im).astype(jnp.bfloat16)

    def finish(tile):
        window = jnp.dot(power_of(tile)[...], band[TILE : 2 * TILE], preferred_element_type=jnp.float32)
        window += jnp.dot(power_of(tile + 1)[...], band[2 * TILE :], preferred_element_type=jnp.float32)
        if tile:
            window += jnp.dot(power_of(tile - 1)[...], band[:TILE], preferred_element_type=jnp.float32)
        bin_index = tile * TILE + lax.broadcasted_iota(jnp.int32, (1, TILE), 1)
        number = jnp.minimum(bin_index + HALF, F - 1) - jnp.maximum(bin_index - HALF, 0) + 1
        inverse = 1.0 / number.astype(jnp.float32)
        at = (tile - max(first - 1, 0)) * 2 * TILE
        for seg in range(segs):
            rows = slice(seg * chans, (seg + 1) * chans)
            scale = lax.rsqrt(window[rows] * inverse + EPSILON)
            scale = jnp.where(eff[...] > seg, scale, 0.0)
            place = slice(seg * half, (seg + 1) * half)
            for lane in (0, TILE):
                white = spectrum_of(tile)[rows, lane : lane + TILE] * scale
                lo, hi = white[:half], white[half:]
                one_ref[place, at + lane : at + lane + TILE] = jnp.where(even, hi, lo).astype(jnp.bfloat16)
                two_ref[place, at + lane : at + lane + TILE] = jnp.where(even, lo, hi).astype(jnp.bfloat16)

    head = max(had, 1)
    stretches = [list(range(first, head))] + [list(range(tile, min(tile + 2, stop))) for tile in range(head, stop, 2)]
    if not first:
        fetch(0).start()
        vectors, load_sems = refs["vectors"], refs["load_sems"]
        loads = []
        for seg in range(segs):
            rows = pl.ds(seg * chans, chans)
            loads.append(pltpu.make_async_copy(refs["x_hbm"].at[rows], x.at[rows], load_sems.at[seg]))
        loads.append(pltpu.make_async_copy(refs["counts_hbm"], vectors.at[0], load_sems.at[segs]))
        loads.append(pltpu.make_async_copy(refs["alive_hbm"], vectors.at[1], load_sems.at[segs + 1]))
        for load in loads:
            load.start()
    row = lax.broadcasted_iota(jnp.int32, (3 * TILE, TILE), 0)
    column = lax.broadcasted_iota(jnp.int32, (3 * TILE, TILE), 1)
    band[...] = (jnp.abs(row - TILE - column) <= HALF).astype(jnp.float32).astype(jnp.bfloat16)

    def limits():
        left = counts[0:1, :] - (lax.axis_index("seg") * segs).astype(jnp.float32)
        eff[...] = jnp.transpose(jnp.broadcast_to(left, (chans, chans)))

    if first:
        limits()
    for index, stretch in enumerate(stretches):
        later = stretches[index + 1] if index + 1 < len(stretches) else range(stop, further)
        for tile in later:
            fetch(tile).start()
        for tile in stretch:
            if tile >= had:
                fetch(tile).wait()
        if not first and index == 0:
            for load in loads:
                load.wait()
        if not first and index == 0:
            counts[0:1] = jnp.where(vectors[1] > 0, vectors[0], 0).astype(jnp.float32)
            counts[1:2] = vectors[0].astype(jnp.float32)
            limits()
            row = jnp.broadcast_to(counts[1:2, :].astype(jnp.bfloat16), (EXTRA, chans))
            for ref in (one_ref, two_ref):
                for lane in range(0, ref.shape[1], chans):
                    ref[segs * half :, lane : lane + chans] = row
        for tile in stretch:
            store(tile)
    for tile in range(max(first - 1, 0), stop - 1):
        finish(tile)
    for tile in range(stop, further):
        fetch(tile).wait()


def held(arrays):
    return [pltpu.with_memory_space_constraint(array, pltpu.VMEM) for array in arrays]


def whiten(plan, given, table, segs, chans):
    first, stop, further, tiles = plan
    total, length = segs * chans, table.shape[2]
    made = stop - first
    done = stop - 1 - max(first - 1, 0)
    send = total // 2 + (0 if first else EXTRA)
    here, away = pl.BlockSpec(memory_space=pltpu.VMEM), pl.BlockSpec(memory_space=pl.ANY)
    outs = {name: pltpu.VMEM((send, 2 * TILE * done), jnp.bfloat16) for name in ("one", "two")}
    handed = {}
    scratch = {
        "spectra": pltpu.VMEM((made, total, 2 * TILE), jnp.float32),
        "power": pltpu.VMEM((made, total, TILE), jnp.bfloat16),
        "band": pltpu.VMEM((3 * TILE, TILE), jnp.bfloat16),
        "eff": pltpu.VMEM((chans, chans), jnp.float32),
        "sems": pltpu.SemaphoreType.DMA((further - first,)),
    }
    lacking = made - (given["table_in"].shape[0] if first else 0)
    if lacking:
        scratch["buffers"] = pltpu.VMEM((lacking, length, 2 * TILE), jnp.bfloat16)
    if not first:
        handed["x"] = pltpu.VMEM((total, length), jnp.bfloat16)
        handed["counts"] = pltpu.VMEM((2, chans), jnp.float32)
        scratch["vectors"] = pltpu.VMEM((2, 1, chans), jnp.int32)
        scratch["load_sems"] = pltpu.SemaphoreType.DMA((segs + 2,))
    if stop <= tiles:
        handed["spectrum_out"] = pltpu.VMEM((total, 2 * TILE), jnp.float32)
        handed["power_out"] = pltpu.VMEM((2, total, TILE), jnp.bfloat16)
        handed["table_out"] = pltpu.VMEM((further - stop, length, 2 * TILE), jnp.bfloat16)
    if first:
        operands = held(given.values())
    else:
        operands = [pltpu.with_memory_space_constraint(array, pltpu.HBM) for array in given.values()]
    names = ["table", *given, *outs, *handed, *scratch]
    results = pl.pallas_call(
        functools.partial(whiten_kernel, plan, names),
        out_shape=[*outs.values(), *handed.values()],
        in_specs=[away] + [here if first else away] * len(operands),
        out_specs=[here] * (len(outs) + len(handed)),
        scratch_shapes=list(scratch.values()),
        compiler_params=pltpu.CompilerParams(vmem_limit_bytes=24 * MIB),
        cost_estimate=pl.CostEstimate(
            flops=2 * total * length * 2 * TILE * made,
            bytes_accessed=2 * length * 2 * TILE * made + 2 * total * length,
            transcendentals=0,
        ),
        name="whiten",
    )(table, *operands)
    handed = dict(zip(handed, results[2:]))
    kept = {name: handed.get(name, given.get(name)) for name in ("x", "counts")}
    passed = {name.replace("_out", "_in"): array for name, array in handed.items() if name.endswith("_out")}
    return results[0], results[1], {**kept, **passed}


def window_start(offset, chans):
    return jnp.minimum(chans // 2, chans - offset) // 16 * 16


def correlate_kernel(plan, offsets, one_ref, two_ref, got_one_ref, got_two_ref, table_hbm, *refs):
    tile_first, is_first, is_last = plan
    refs = list(refs)
    earlier = refs.pop(0)
    if is_last:
        keep_ref, send_ref = refs.pop(0), refs.pop(0)
    else:
        total = refs.pop(0)
    if is_first:
        inverse_ref = refs.pop(0)
    if is_last:
        total = refs.pop(0)
    select, frame, far, cross, delay, sems = refs
    tiles, segs, span, _ = frame.shape
    chans, half = span // 2, span // 4
    slots = cross.shape[0] // chans
    parts, depth, width = delay.shape
    last_place, length = table_hbm.shape[1] - 1, table_hbm.shape[2] // parts
    place = lax.axis_index("chan")
    even = place & 1 == 0
    known = jnp.where(place < lax.axis_size("chan") - 1, 4 * half, 3 * half)

    copies = []
    for part in range(parts):
        rows = pl.ds(part * length + tile_first * 2 * TILE, depth)
        source = table_hbm.at[lax.axis_index("freq"), last_place, rows, :]
        copies.append(pltpu.make_async_copy(source, delay.at[part], sems.at[part]))
        copies[part].start()

    row = lax.broadcasted_iota(jnp.int32, (chans, 2 * chans), 0)
    column = lax.broadcasted_iota(jnp.int32, (chans, 2 * chans), 1)
    for slot in range(slots):
        offset = offsets[slot]
        match = (column == row + window_start(offset, chans) + offset) & (column < known)
        select[slot * chans : (slot + 1) * chans] = match.astype(jnp.float32).astype(jnp.bfloat16)
    if is_first:
        row = lax.broadcasted_iota(jnp.int32, (chans, chans), 0)
        column = lax.broadcasted_iota(jnp.int32, (chans, chans), 1)
        own = earlier[1:2, :]
        following = [ref[segs * half :, :chans].astype(jnp.float32)[:1] for ref in (got_one_ref, got_two_ref)]
        following = jnp.where(even, *following)
        mine = jnp.sum(jnp.where(row == column, own, 0.0), axis=1, keepdims=True)
        for slot in range(slots):
            target = row + offsets[slot]
            partner = jnp.where(column == target, own, 0.0) + jnp.where(column + chans == target, following, 0.0)
            partner = jnp.sum(partner, axis=1, keepdims=True)
            divisor = jnp.maximum(jnp.minimum(mine, partner), 1.0)
            inverse_ref[slot] = jnp.broadcast_to(1.0 / divisor, inverse_ref.shape[1:])
    if is_last:
        keep_ref[...] = jnp.zeros_like(keep_ref)
        send_ref[...] = jnp.zeros_like(send_ref)

    order = ((one_ref, 2, 1), (two_ref, 1, 2), (got_one_ref, 3, 0), (got_two_ref, 0, 3))
    done = 0
    for tile in range(tiles):
        for ref, if_even, if_odd in order:
            spot = pl.ds(pl.multiple_of(jnp.where(even, if_even * half, if_odd * half), half), half)
            for seg in range(segs):
                rows = slice(seg * half, (seg + 1) * half)
                frame[tile, seg, spot, :] = ref[rows, tile * 2 * TILE : (tile + 1) * 2 * TILE]
        turn = tile % far.shape[0]
        for seg in range(segs):
            far[turn, seg] = jnp.dot(select[...], frame[tile, seg], preferred_element_type=jnp.float32)
        for slot in range(slots):
            start = window_start(offsets[slot], chans)
            for index in range(chans // 16):
                real = jnp.zeros((16, TILE), jnp.float32)
                imag = jnp.zeros((16, TILE), jnp.float32)
                base = pl.multiple_of(start + index * 16, 16)
                spot = slice(slot * chans + index * 16, slot * chans + index * 16 + 16)
                for seg in range(segs):
                    own = frame[tile, seg, pl.ds(base, 16), :].astype(jnp.float32)
                    own_re, own_im = own[:, :TILE], own[:, TILE:]
                    far_re, far_im = far[turn, seg, spot, :TILE], far[turn, seg, spot, TILE:]
                    real += own_re * far_re + own_im * far_im
                    imag += own_im * far_re - own_re * far_im
                lane = tile * 2 * TILE
                cross[spot, lane : lane + TILE] = real.astype(jnp.bfloat16)
                cross[spot, lane + TILE : lane + 2 * TILE] = imag.astype(jnp.bfloat16)
        if tile + 1 < tiles and (tile + 1) % LAG_TILES:
            continue
        lanes = slice(done * 2 * TILE, (tile + 1) * 2 * TILE)
        for part in range(parts):
            if not done:
                copies[part].wait()
            for slot in range(slots):
                spot, columns = slice(slot * chans, (slot + 1) * chans), slice(part * width, (part + 1) * width)
                term = jnp.dot(cross[spot, lanes], delay[part, lanes], preferred_element_type=jnp.float32)
                if done:
                    term += total[spot, columns]
                elif not is_first:
                    term += earlier[spot, columns]
                if not is_last or tile + 1 < tiles:
                    total[spot, columns] = term
                    continue
                rows = pl.ds(pl.multiple_of(window_start(offsets[slot], chans), 16), chans)
                if part == 0:
                    keep_ref[slot, rows, :] = term
                else:
                    send_ref[slot, rows, (part - 1) * width : part * width] = term.astype(send_ref.dtype)
        done = tile + 1


def correlate(plan, offsets, sent, got, table, earlier, segs, chans):
    tile_first, is_first, is_last = plan
    half, columns = chans // 2, sent[0].shape[1]
    tiles = columns // (2 * TILE)
    slots = offsets.shape[0]
    parts, keep = table.shape[0], table.shape[3]
    lags = parts * keep
    here = pl.BlockSpec(memory_space=pltpu.VMEM)
    scratch = [
        pltpu.VMEM((slots * chans, 2 * chans), jnp.bfloat16),
        pltpu.VMEM((tiles, segs, 2 * chans, 2 * TILE), jnp.bfloat16),
        pltpu.VMEM((2, segs, slots * chans, 2 * TILE), jnp.float32),
        pltpu.VMEM((slots * chans, columns), jnp.bfloat16),
        pltpu.VMEM((parts, columns, keep), jnp.bfloat16),
        pltpu.SemaphoreType.DMA((parts,)),
    ]
    if is_last:
        out_shape = [
            pltpu.VMEM((slots, 3 * half, keep), jnp.float32),
            pltpu.VMEM((slots, 3 * half, lags - keep), jnp.bfloat16),
        ]
        scratch = [pltpu.VMEM((slots * chans, lags), jnp.float32)] + scratch
    else:
        out_shape = [pltpu.VMEM((slots * chans, lags), jnp.float32)]
    if is_first:
        out_shape += [pltpu.VMEM((slots, chans, keep), jnp.float32)]
    return pl.pallas_call(
        functools.partial(correlate_kernel, plan),
        out_shape=out_shape,
        grid_spec=pltpu.PrefetchScalarGridSpec(
            num_scalar_prefetch=1,
            grid=(),
            in_specs=[here] * 4 + [pl.BlockSpec(memory_space=pl.ANY), here],
            out_specs=[here] * len(out_shape),
            scratch_shapes=scratch,
        ),
        compiler_params=pltpu.CompilerParams(vmem_limit_bytes=20 * MIB),
        cost_estimate=pl.CostEstimate(
            flops=tiles * 2 * slots * chans * 2 * TILE * (segs * 2 * chans + lags),
            bytes_accessed=tiles * (4 * segs * half * 2 * TILE * 2),
            transcendentals=0,
        ),
        name="correlate",
    )(offsets, *held([*sent, *got]), table, *held([earlier]))


def swap(block, first):
    blocks, parts = lax.axis_size("chan"), lax.axis_size("freq")
    route = []
    for i in range(blocks):
        partner = i + 1 if (i - first) % 2 == 0 else i - 1
        alone = not 0 <= partner < blocks
        for part in range(parts):
            target = i * parts + (part + 1) % parts if alone else partner * parts + part
            route.append((i * parts + part, target))
    return lax.ppermute(block, ("chan", "freq"), route)


def returns(blocks, parts):
    near, far = {}, {}
    last = blocks - 1
    for i in range(blocks):
        near[i, 1] = (i - 1, 1) if i else (0, 0)
        near[i, 0] = (i + 1, 0) if i < last else (last, 1)
        far[i, 0] = (i - 1, 1) if i else (0, 0)
        far[i, 1] = (i + 1, 0) if i < last else (last, 1)
    routes = []
    for steps in (near, far):
        route = []
        for source, target in steps.items():
            for part in range(parts):
                end = (part + 1) % parts if source == target else part
                route.append(((2 * source[0] + source[1]) * parts + part, (2 * target[0] + target[1]) * parts + end))
        routes.append(route)
    return routes


def reduced(span, keep, chans, has_next):
    spans, blocks = lax.axis_size("seg"), lax.axis_size("chan")
    half = chans // 2
    back = lax.ppermute(keep[:, :half].astype(jnp.bfloat16), "chan", [(i, (i - 1) % blocks) for i in range(blocks)])
    back = jnp.where(has_next, back.astype(jnp.float32), 0.0)
    keep = keep[:, half:] + jnp.pad(back, ((0, 0), (chans - half, 0), (0, 0)))
    piece = chans // spans
    result = lax.dynamic_slice_in_dim(keep, span * piece, piece, 1)
    for step in range(1, spans):
        target = lax.rem(span + step, spans)
        block = lax.dynamic_slice_in_dim(keep, target * piece, piece, 1).astype(jnp.bfloat16)
        block = lax.ppermute(block, "seg", [(i, (i + step) % spans) for i in range(spans)])
        result = result + block.astype(jnp.float32)
    return result


def shards(traces, dead_mask, seg_counts, offsets):
    segs, chans, length = traces.shape
    half = chans // 2
    parts, spans, blocks = lax.axis_size("freq"), lax.axis_size("seg"), lax.axis_size("chan")
    assert parts == 2
    table = jnp.asarray(tables(length, parts))
    tiles = table.shape[1] - 2
    span = lax.axis_index("seg").astype(jnp.int32)
    has_next = lax.axis_index("chan") < blocks - 1
    given = {
        "x_hbm": traces.reshape(segs * chans, length),
        "counts_hbm": seg_counts.reshape(1, chans),
        "alive_hbm": dead_mask.reshape(1, chans),
    }
    groups, made = [], 0
    for stop, further in zip(GROUPS, AHEAD):
        one, two, given = whiten((made, stop, further, tiles), given, table, segs, chans)
        groups.append((max(made - 1, 0), segs, (one, two), (swap(one, 0), swap(two, 1))))
        made = stop
    earlier = given["counts"]
    for index, (tile_first, number, sent, got) in enumerate(groups):
        plan = (tile_first, index == 0, index == len(groups) - 1)
        results = list(correlate(plan, offsets, sent, got, table, earlier, number, chans))
        if index == 0:
            inverse = results.pop()
        earlier = results[0]
    keep, send = results
    keep = keep + lax.ppermute(send, "freq", [(0, 1), (1, 0)]).astype(jnp.float32)
    if spans == 2:
        lower, upper = keep[:, half:chans], keep[:, chans:]
        mine = jnp.where(span == 0, lower, upper)
        other = jnp.where(span == 0, upper, lower).astype(jnp.bfloat16)
        back = keep[:, :half].astype(jnp.bfloat16)
        other = lax.ppermute(other, "seg", [(0, 1), (1, 0)])
        route_near, route_far = returns(blocks, parts)
        near = lax.ppermute(back, ("chan", "seg", "freq"), route_near)
        far = lax.ppermute(back, ("chan", "seg", "freq"), route_far)
        returned = jnp.where(has_next & (span == 1), near.astype(jnp.float32) + far.astype(jnp.float32), 0.0)
        result = mine + other.astype(jnp.float32) + returned
        result = result * jnp.where(span == 0, inverse[:, :half], inverse[:, half:])
    else:
        piece = chans // spans
        result = reduced(span, keep, chans, has_next)
        result = result * lax.dynamic_slice_in_dim(inverse, span * piece, piece, 1)
    return jnp.transpose(result, (1, 0, 2))


def solution(mesh):
    in_specs = (
        P("seg", ("groups", "chan"), None),
        P(("groups", "chan")),
        P(("groups", "chan")),
        P(),
    )
    out_specs = P(("groups", "chan", "seg"), None, "freq")
    return jax.shard_map(shards, mesh=mesh, in_specs=in_specs, out_specs=out_specs, check_vma=False)
```

```python
import functools
import math

import jax
import jax.numpy as jnp
import numpy as np
from jax import lax
from jax.experimental import pallas as pl
from jax.experimental.pallas import tpu as pltpu
from jax.sharding import PartitionSpec as P
import ml_dtypes

HALF = 32
LAGS = 512
F = 2048
TILE = 128
EPSILON = 1e-06
MIB = 1 << 20
EXTRA = 16
LAG_TILES = 4
GROUPS = (4, 7, 9)
AHEAD = (5, 8, 9)


def tables(length, parts):
    bins_dev = F // parts
    tiles = bins_dev // TILE
    cosines = np.cos(np.arange(length) * (2.0 * math.pi / length))
    sines = -np.sin(np.arange(length) * (2.0 * math.pi / length))
    cos16 = cosines.astype(np.float32).astype(ml_dtypes.bfloat16)
    sin16 = sines.astype(np.float32).astype(ml_dtypes.bfloat16)
    samples = np.arange(length)[:, None]
    fourier = np.zeros((parts, tiles + 2, length, 2 * TILE), ml_dtypes.bfloat16)
    lag_part = LAGS // parts
    delay = np.zeros((2 * bins_dev, LAGS), ml_dtypes.bfloat16)
    scaling = 1.0 / math.sqrt(F)
    for part in range(parts):
        shifts = np.roll(np.arange(LAGS), -part * lag_part) - LAGS // 2
        for tile in range(tiles + 1):
            place = tile * TILE + np.arange(TILE)
            bin_index = F - 1 - place if part else place
            phases = samples * bin_index[None, :] % length
            width = TILE if tile < tiles else HALF
            fourier[part, tile, :, :width] = cos16[phases[:, :width]]
            fourier[part, tile, :, TILE : TILE + width] = sin16[phases[:, :width]]
            if tile < tiles:
                phases = bin_index[:, None] * shifts[None, :] % length
                rows = tile * 2 * TILE
                delay[rows : rows + TILE] = (cosines[phases] * scaling).astype(ml_dtypes.bfloat16)
                delay[rows + TILE : rows + 2 * TILE] = (sines[phases] * scaling).astype(ml_dtypes.bfloat16)
        blocks = delay.reshape(tiles, 2 * TILE, parts, lag_part).transpose(2, 0, 1, 3)
        fourier[part, tiles + 1, : tiles * parts * 2 * TILE, :lag_part] = blocks.reshape(-1, lag_part)
    return fourier


def whiten_kernel(plan, names, *refs):
    first, stop, further, tiles = plan
    refs = dict(zip(names, refs))
    x, counts, table_hbm = refs["x"], refs["counts"], refs["table"]
    one_ref, two_ref, eff, band, sems = (refs[name] for name in ("one", "two", "eff", "band", "sems"))
    chans = eff.shape[0]
    total, length = x.shape
    segs, half = total // chans, chans // 2
    even = lax.axis_index("chan") & 1 == 0
    buffers, had = refs.get("buffers"), first + (refs["table_in"].shape[0] if "table_in" in refs else 0)

    def fetch(tile):
        source = table_hbm.at[lax.axis_index("freq"), tile]
        target = refs["table_out"].at[tile - stop] if tile >= stop else buffers.at[tile - had]
        return pltpu.make_async_copy(source, target, sems.at[tile - first])

    def table_of(tile):
        return refs["table_in"].at[tile - first] if tile < had else buffers.at[tile - had]

    def spectrum_of(tile):
        if tile < first:
            return refs["spectrum_in"]
        return refs["spectrum_out"] if tile == stop - 1 <= tiles - 1 else refs["spectra"].at[tile - first]

    def power_of(tile):
        if tile < first:
            return refs["power_in"].at[tile - first + 2]
        return refs["power_out"].at[tile - stop + 2] if stop - 2 <= tile and stop <= tiles else refs["power"].at[tile - first]

    def store(tile, rows):
        block = jnp.dot(x[rows], table_of(tile)[...], preferred_element_type=jnp.float32)
        spectrum_of(tile)[rows] = block
        re, im = block[:, :TILE], block[:, TILE:]
        power_of(tile)[rows] = (re * re + im * im).astype(jnp.bfloat16)

    def finish(tile):
        window = jnp.dot(power_of(tile)[...], band[TILE : 2 * TILE], preferred_element_type=jnp.float32)
        window += jnp.dot(power_of(tile + 1)[...], band[2 * TILE :], preferred_element_type=jnp.float32)
        if tile:
            window += jnp.dot(power_of(tile - 1)[...], band[:TILE], preferred_element_type=jnp.float32)
        bin_index = tile * TILE + lax.broadcasted_iota(jnp.int32, (1, TILE), 1)
        number = jnp.minimum(bin_index + HALF, F - 1) - jnp.maximum(bin_index - HALF, 0) + 1
        inverse = 1.0 / number.astype(jnp.float32)
        at = (tile - max(first - 1, 0)) * 2 * TILE
        for seg in range(segs):
            rows = slice(seg * chans, (seg + 1) * chans)
            scale = lax.rsqrt(window[rows] * inverse + EPSILON)
            scale = jnp.where(eff[...] > seg, scale, 0.0)
            place = slice(seg * half, (seg + 1) * half)
            for lane in (0, TILE):
                white = spectrum_of(tile)[rows, lane : lane + TILE] * scale
                lo, hi = white[:half], white[half:]
                one_ref[place, at + lane : at + lane + TILE] = jnp.where(even, hi, lo).astype(jnp.bfloat16)
                two_ref[place, at + lane : at + lane + TILE] = jnp.where(even, lo, hi).astype(jnp.bfloat16)

    rows = slice(0, total)
    if first:
        head = max(had, first + 1)
        own = [fetch(tile) for tile in range(had, head)]
        stretches = [(own, [(tile, rows) for tile in range(first, head)])]
    else:
        head = 2
        vectors, load_sems = refs["vectors"], refs["load_sems"]
        early = (segs + 1) // 2
        loads = []
        for seg in range(segs):
            place = pl.ds(seg * chans, chans)
            loads.append(pltpu.make_async_copy(refs["x_hbm"].at[place], x.at[place], load_sems.at[seg]))
        whole = [
            pltpu.make_async_copy(refs["counts_hbm"], vectors.at[0], load_sems.at[segs]),
            pltpu.make_async_copy(refs["alive_hbm"], vectors.at[1], load_sems.at[segs + 1]),
        ]
        stretches = [
            ([fetch(0), *loads[:early], *whole], [(0, slice(0, early * chans))]),
            ([*loads[early:], fetch(1)], [(0, slice(early * chans, total)), (1, rows)]),
        ]
    if (stop - head) % 2:
        stretches.append(([fetch(head)], [(head, rows)]))
        head += 1
    for tile in range(head, stop, 2):
        stretches.append(([fetch(tile), fetch(tile + 1)], [(tile, rows), (tile + 1, rows)]))
    stretches.append(([fetch(tile) for tile in range(stop, further)], []))
    for copy in stretches[0][0]:
        copy.start()
    row = lax.broadcasted_iota(jnp.int32, (3 * TILE, TILE), 0)
    column = lax.broadcasted_iota(jnp.int32, (3 * TILE, TILE), 1)
    band[...] = (jnp.abs(row - TILE - column) <= HALF).astype(jnp.float32).astype(jnp.bfloat16)

    def limits():
        left = counts[0:1, :] - (lax.axis_index("seg") * segs).astype(jnp.float32)
        eff[...] = jnp.transpose(jnp.broadcast_to(left, (chans, chans)))

    if first:
        limits()
    for index, (copies, products) in enumerate(stretches[:-1]):
        for copy in stretches[index + 1][0]:
            copy.start()
        for copy in copies:
            copy.wait()
        if not first and index == 0:
            counts[0:1] = jnp.where(vectors[1] > 0, vectors[0], 0).astype(jnp.float32)
            counts[1:2] = vectors[0].astype(jnp.float32)
            limits()
            row = jnp.broadcast_to(counts[1:2, :].astype(jnp.bfloat16), (EXTRA, chans))
            for ref in (one_ref, two_ref):
                for lane in range(0, ref.shape[1], chans):
                    ref[segs * half :, lane : lane + chans] = row
        for product in products:
            store(*product)
    for tile in range(max(first - 1, 0), stop - 1):
        finish(tile)
    for copy in stretches[-1][0]:
        copy.wait()


def held(arrays):
    return [pltpu.with_memory_space_constraint(array, pltpu.VMEM) for array in arrays]


def whiten(plan, given, table, segs, chans):
    first, stop, further, tiles = plan
    total, length = segs * chans, table.shape[2]
    made = stop - first
    done = stop - 1 - max(first - 1, 0)
    send = total // 2 + (0 if first else EXTRA)
    here, away = pl.BlockSpec(memory_space=pltpu.VMEM), pl.BlockSpec(memory_space=pl.ANY)
    outs = {name: pltpu.VMEM((send, 2 * TILE * done), jnp.bfloat16) for name in ("one", "two")}
    handed = {}
    scratch = {
        "spectra": pltpu.VMEM((made, total, 2 * TILE), jnp.float32),
        "power": pltpu.VMEM((made, total, TILE), jnp.bfloat16),
        "band": pltpu.VMEM((3 * TILE, TILE), jnp.bfloat16),
        "eff": pltpu.VMEM((chans, chans), jnp.float32),
        "sems": pltpu.SemaphoreType.DMA((max(further, stop) - first,)),
    }
    lacking = made - (given["table_in"].shape[0] if "table_in" in given else 0)
    if lacking:
        scratch["buffers"] = pltpu.VMEM((lacking, length, 2 * TILE), jnp.bfloat16)
    if not first:
        handed["x"] = pltpu.VMEM((total, length), jnp.bfloat16)
        handed["counts"] = pltpu.VMEM((2, chans), jnp.float32)
        scratch["vectors"] = pltpu.VMEM((2, 1, chans), jnp.int32)
        scratch["load_sems"] = pltpu.SemaphoreType.DMA((segs + 2,))
    if stop <= tiles:
        handed["spectrum_out"] = pltpu.VMEM((total, 2 * TILE), jnp.float32)
        handed["power_out"] = pltpu.VMEM((2, total, TILE), jnp.bfloat16)
    if further > stop:
        handed["table_out"] = pltpu.VMEM((further - stop, length, 2 * TILE), jnp.bfloat16)
    if first:
        operands = held(given.values())
    else:
        operands = [pltpu.with_memory_space_constraint(array, pltpu.HBM) for array in given.values()]
    names = ["table", *given, *outs, *handed, *scratch]
    results = pl.pallas_call(
        functools.partial(whiten_kernel, plan, names),
        out_shape=[*outs.values(), *handed.values()],
        in_specs=[away] + [here if first else away] * len(operands),
        out_specs=[here] * (len(outs) + len(handed)),
        scratch_shapes=list(scratch.values()),
        compiler_params=pltpu.CompilerParams(vmem_limit_bytes=24 * MIB),
        cost_estimate=pl.CostEstimate(
            flops=2 * total * length * 2 * TILE * made,
            bytes_accessed=2 * length * 2 * TILE * made + 2 * total * length,
            transcendentals=0,
        ),
        name="whiten",
    )(table, *operands)
    handed = dict(zip(handed, results[2:]))
    kept = {name: handed.get(name, given.get(name)) for name in ("x", "counts")}
    passed = {name.replace("_out", "_in"): array for name, array in handed.items() if name.endswith("_out")}
    return results[0], results[1], {**kept, **passed}


def window_start(offset, chans):
    return jnp.minimum(chans // 2, chans - offset) // 16 * 16


def correlate_kernel(plan, offsets, one_ref, two_ref, got_one_ref, got_two_ref, table_hbm, *refs):
    tile_first, is_first, is_last = plan
    refs = list(refs)
    earlier = refs.pop(0)
    if is_last:
        keep_ref, send_ref = refs.pop(0), refs.pop(0)
    else:
        total = refs.pop(0)
    if is_first:
        inverse_ref = refs.pop(0)
    if is_last:
        total = refs.pop(0)
    select, frame, far, cross, delay, sems = refs
    tiles, segs, span, _ = frame.shape
    chans, half = span // 2, span // 4
    slots = cross.shape[0] // chans
    parts, depth, width = delay.shape
    last_place, length = table_hbm.shape[1] - 1, table_hbm.shape[2] // parts
    place = lax.axis_index("chan")
    even = place & 1 == 0
    known = jnp.where(place < lax.axis_size("chan") - 1, 4 * half, 3 * half)

    copies = []
    for part in range(parts):
        rows = pl.ds(part * length + tile_first * 2 * TILE, depth)
        source = table_hbm.at[lax.axis_index("freq"), last_place, rows, :]
        copies.append(pltpu.make_async_copy(source, delay.at[part], sems.at[part]))
        copies[part].start()

    row = lax.broadcasted_iota(jnp.int32, (chans, 2 * chans), 0)
    column = lax.broadcasted_iota(jnp.int32, (chans, 2 * chans), 1)
    for slot in range(slots):
        offset = offsets[slot]
        match = (column == row + window_start(offset, chans) + offset) & (column < known)
        select[slot * chans : (slot + 1) * chans] = match.astype(jnp.float32).astype(jnp.bfloat16)
    if is_first:
        row = lax.broadcasted_iota(jnp.int32, (chans, chans), 0)
        column = lax.broadcasted_iota(jnp.int32, (chans, chans), 1)
        own = earlier[1:2, :]
        following = [ref[segs * half :, :chans].astype(jnp.float32)[:1] for ref in (got_one_ref, got_two_ref)]
        following = jnp.where(even, *following)
        mine = jnp.sum(jnp.where(row == column, own, 0.0), axis=1, keepdims=True)
        for slot in range(slots):
            target = row + offsets[slot]
            partner = jnp.where(column == target, own, 0.0) + jnp.where(column + chans == target, following, 0.0)
            partner = jnp.sum(partner, axis=1, keepdims=True)
            divisor = jnp.maximum(jnp.minimum(mine, partner), 1.0)
            inverse_ref[slot] = jnp.broadcast_to(1.0 / divisor, inverse_ref.shape[1:])
    if is_last:
        keep_ref[...] = jnp.zeros_like(keep_ref)
        send_ref[...] = jnp.zeros_like(send_ref)

    order = ((one_ref, 2, 1), (two_ref, 1, 2), (got_one_ref, 3, 0), (got_two_ref, 0, 3))
    done = 0
    for tile in range(tiles):
        for ref, if_even, if_odd in order:
            spot = pl.ds(pl.multiple_of(jnp.where(even, if_even * half, if_odd * half), half), half)
            for seg in range(segs):
                rows = slice(seg * half, (seg + 1) * half)
                frame[tile, seg, spot, :] = ref[rows, tile * 2 * TILE : (tile + 1) * 2 * TILE]
        turn = tile % far.shape[0]
        for seg in range(segs):
            far[turn, seg] = jnp.dot(select[...], frame[tile, seg], preferred_element_type=jnp.float32)
        for slot in range(slots):
            start = window_start(offsets[slot], chans)
            for index in range(chans // 16):
                real = jnp.zeros((16, TILE), jnp.float32)
                imag = jnp.zeros((16, TILE), jnp.float32)
                base = pl.multiple_of(start + index * 16, 16)
                spot = slice(slot * chans + index * 16, slot * chans + index * 16 + 16)
                for seg in range(segs):
                    own = frame[tile, seg, pl.ds(base, 16), :].astype(jnp.float32)
                    own_re, own_im = own[:, :TILE], own[:, TILE:]
                    far_re, far_im = far[turn, seg, spot, :TILE], far[turn, seg, spot, TILE:]
                    real += own_re * far_re + own_im * far_im
                    imag += own_im * far_re - own_re * far_im
                lane = tile * 2 * TILE
                cross[spot, lane : lane + TILE] = real.astype(jnp.bfloat16)
                cross[spot, lane + TILE : lane + 2 * TILE] = imag.astype(jnp.bfloat16)
        if tile + 1 < tiles and (tile + 1) % LAG_TILES:
            continue
        lanes = slice(done * 2 * TILE, (tile + 1) * 2 * TILE)
        for part in range(parts):
            if not done:
                copies[part].wait()
            for slot in range(slots):
                spot, columns = slice(slot * chans, (slot + 1) * chans), slice(part * width, (part + 1) * width)
                term = jnp.dot(cross[spot, lanes], delay[part, lanes], preferred_element_type=jnp.float32)
                if done:
                    term += total[spot, columns]
                elif not is_first:
                    term += earlier[spot, columns]
                if not is_last or tile + 1 < tiles:
                    total[spot, columns] = term
                    continue
                rows = pl.ds(pl.multiple_of(window_start(offsets[slot], chans), 16), chans)
                if part == 0:
                    keep_ref[slot, rows, :] = term
                else:
                    send_ref[slot, rows, (part - 1) * width : part * width] = term.astype(send_ref.dtype)
        done = tile + 1


def correlate(plan, offsets, sent, got, table, earlier, segs, chans):
    tile_first, is_first, is_last = plan
    half, columns = chans // 2, sent[0].shape[1]
    tiles = columns // (2 * TILE)
    slots = offsets.shape[0]
    parts, keep = table.shape[0], table.shape[3]
    lags = parts * keep
    here = pl.BlockSpec(memory_space=pltpu.VMEM)
    scratch = [
        pltpu.VMEM((slots * chans, 2 * chans), jnp.bfloat16),
        pltpu.VMEM((tiles, segs, 2 * chans, 2 * TILE), jnp.bfloat16),
        pltpu.VMEM((2, segs, slots * chans, 2 * TILE), jnp.float32),
        pltpu.VMEM((slots * chans, columns), jnp.bfloat16),
        pltpu.VMEM((parts, columns, keep), jnp.bfloat16),
        pltpu.SemaphoreType.DMA((parts,)),
    ]
    if is_last:
        out_shape = [
            pltpu.VMEM((slots, 3 * half, keep), jnp.float32),
            pltpu.VMEM((slots, 3 * half, lags - keep), jnp.bfloat16),
        ]
        scratch = [pltpu.VMEM((slots * chans, lags), jnp.float32)] + scratch
    else:
        out_shape = [pltpu.VMEM((slots * chans, lags), jnp.float32)]
    if is_first:
        out_shape += [pltpu.VMEM((slots, chans, keep), jnp.float32)]
    return pl.pallas_call(
        functools.partial(correlate_kernel, plan),
        out_shape=out_shape,
        grid_spec=pltpu.PrefetchScalarGridSpec(
            num_scalar_prefetch=1,
            grid=(),
            in_specs=[here] * 4 + [pl.BlockSpec(memory_space=pl.ANY), here],
            out_specs=[here] * len(out_shape),
            scratch_shapes=scratch,
        ),
        compiler_params=pltpu.CompilerParams(vmem_limit_bytes=20 * MIB),
        cost_estimate=pl.CostEstimate(
            flops=tiles * 2 * slots * chans * 2 * TILE * (segs * 2 * chans + lags),
            bytes_accessed=tiles * (4 * segs * half * 2 * TILE * 2),
            transcendentals=0,
        ),
        name="correlate",
    )(offsets, *held([*sent, *got]), table, *held([earlier]))


def swap(block, first):
    blocks, parts = lax.axis_size("chan"), lax.axis_size("freq")
    route = []
    for i in range(blocks):
        partner = i + 1 if (i - first) % 2 == 0 else i - 1
        alone = not 0 <= partner < blocks
        for part in range(parts):
            target = i * parts + (part + 1) % parts if alone else partner * parts + part
            route.append((i * parts + part, target))
    return lax.ppermute(block, ("chan", "freq"), route)


def returns(blocks, parts):
    near, far = {}, {}
    last = blocks - 1
    for i in range(blocks):
        near[i, 1] = (i - 1, 1) if i else (0, 0)
        near[i, 0] = (i + 1, 0) if i < last else (last, 1)
        far[i, 0] = (i - 1, 1) if i else (0, 0)
        far[i, 1] = (i + 1, 0) if i < last else (last, 1)
    routes = []
    for steps in (near, far):
        route = []
        for source, target in steps.items():
            for part in range(parts):
                end = (part + 1) % parts if source == target else part
                route.append(((2 * source[0] + source[1]) * parts + part, (2 * target[0] + target[1]) * parts + end))
        routes.append(route)
    return routes


def reduced(span, keep, chans, has_next):
    spans, blocks = lax.axis_size("seg"), lax.axis_size("chan")
    half = chans // 2
    back = lax.ppermute(keep[:, :half].astype(jnp.bfloat16), "chan", [(i, (i - 1) % blocks) for i in range(blocks)])
    back = jnp.where(has_next, back.astype(jnp.float32), 0.0)
    keep = keep[:, half:] + jnp.pad(back, ((0, 0), (chans - half, 0), (0, 0)))
    piece = chans // spans
    result = lax.dynamic_slice_in_dim(keep, span * piece, piece, 1)
    for step in range(1, spans):
        target = lax.rem(span + step, spans)
        block = lax.dynamic_slice_in_dim(keep, target * piece, piece, 1).astype(jnp.bfloat16)
        block = lax.ppermute(block, "seg", [(i, (i + step) % spans) for i in range(spans)])
        result = result + block.astype(jnp.float32)
    return result


def shards(traces, dead_mask, seg_counts, offsets):
    segs, chans, length = traces.shape
    half = chans // 2
    parts, spans, blocks = lax.axis_size("freq"), lax.axis_size("seg"), lax.axis_size("chan")
    assert parts == 2
    table = jnp.asarray(tables(length, parts))
    tiles = table.shape[1] - 2
    span = lax.axis_index("seg").astype(jnp.int32)
    has_next = lax.axis_index("chan") < blocks - 1
    given = {
        "x_hbm": traces.reshape(segs * chans, length),
        "counts_hbm": seg_counts.reshape(1, chans),
        "alive_hbm": dead_mask.reshape(1, chans),
    }
    groups, made = [], 0
    for stop, further in zip(GROUPS, AHEAD):
        one, two, given = whiten((made, stop, further, tiles), given, table, segs, chans)
        groups.append((max(made - 1, 0), segs, (one, two), (swap(one, 0), swap(two, 1))))
        made = stop
    earlier = given["counts"]
    for index, (tile_first, number, sent, got) in enumerate(groups):
        plan = (tile_first, index == 0, index == len(groups) - 1)
        results = list(correlate(plan, offsets, sent, got, table, earlier, number, chans))
        if index == 0:
            inverse = results.pop()
        earlier = results[0]
    keep, send = results
    keep = keep + lax.ppermute(send, "freq", [(0, 1), (1, 0)]).astype(jnp.float32)
    if spans == 2:
        lower, upper = keep[:, half:chans], keep[:, chans:]
        mine = jnp.where(span == 0, lower, upper)
        other = jnp.where(span == 0, upper, lower).astype(jnp.bfloat16)
        back = keep[:, :half].astype(jnp.bfloat16)
        other = lax.ppermute(other, "seg", [(0, 1), (1, 0)])
        route_near, route_far = returns(blocks, parts)
        near = lax.ppermute(back, ("chan", "seg", "freq"), route_near)
        far = lax.ppermute(back, ("chan", "seg", "freq"), route_far)
        returned = jnp.where(has_next & (span == 1), near.astype(jnp.float32) + far.astype(jnp.float32), 0.0)
        result = mine + other.astype(jnp.float32) + returned
        result = result * jnp.where(span == 0, inverse[:, :half], inverse[:, half:])
    else:
        piece = chans // spans
        result = reduced(span, keep, chans, has_next)
        result = result * lax.dynamic_slice_in_dim(inverse, span * piece, piece, 1)
    return jnp.transpose(result, (1, 0, 2))


def solution(mesh):
    in_specs = (
        P("seg", ("groups", "chan"), None),
        P(("groups", "chan")),
        P(("groups", "chan")),
        P(),
    )
    out_specs = P(("groups", "chan", "seg"), None, "freq")
    return jax.shard_map(shards, mesh=mesh, in_specs=in_specs, out_specs=out_specs, check_vma=False)
```

```python
import functools
import math

import jax
import jax.numpy as jnp
import numpy as np
from jax import lax
from jax.experimental import pallas as pl
from jax.experimental.pallas import tpu as pltpu
from jax.sharding import PartitionSpec as P
import ml_dtypes

HALF = 32
LAGS = 512
F = 2048
TILE = 128
EPSILON = 1e-06
MIB = 1 << 20
EXTRA = 16
LAG_TILES = 1
GROUPS = (4, 7, 9)
AHEAD = (5, 8, 9)


def tables(length, parts):
    bins_dev = F // parts
    tiles = bins_dev // TILE
    cosines = np.cos(np.arange(length) * (2.0 * math.pi / length))
    sines = -np.sin(np.arange(length) * (2.0 * math.pi / length))
    cos16 = cosines.astype(np.float32).astype(ml_dtypes.bfloat16)
    sin16 = sines.astype(np.float32).astype(ml_dtypes.bfloat16)
    samples = np.arange(length)[:, None]
    fourier = np.zeros((parts, tiles + 2, length, 2 * TILE), ml_dtypes.bfloat16)
    lag_part = LAGS // parts
    delay = np.zeros((2 * bins_dev, LAGS), ml_dtypes.bfloat16)
    scaling = 1.0 / math.sqrt(F)
    for part in range(parts):
        shifts = np.roll(np.arange(LAGS), -part * lag_part) - LAGS // 2
        for tile in range(tiles + 1):
            place = tile * TILE + np.arange(TILE)
            bin_index = F - 1 - place if part else place
            phases = samples * bin_index[None, :] % length
            width = TILE if tile < tiles else HALF
            fourier[part, tile, :, :width] = cos16[phases[:, :width]]
            fourier[part, tile, :, TILE : TILE + width] = sin16[phases[:, :width]]
            if tile < tiles:
                phases = bin_index[:, None] * shifts[None, :] % length
                rows = tile * 2 * TILE
                delay[rows : rows + TILE] = (cosines[phases] * scaling).astype(ml_dtypes.bfloat16)
                delay[rows + TILE : rows + 2 * TILE] = (sines[phases] * scaling).astype(ml_dtypes.bfloat16)
        blocks = delay.reshape(tiles, 2 * TILE, parts, lag_part).transpose(2, 0, 1, 3)
        fourier[part, tiles + 1, : tiles * parts * 2 * TILE, :lag_part] = blocks.reshape(-1, lag_part)
    return fourier


def whiten_kernel(plan, names, *refs):
    first, stop, further, tiles = plan
    refs = dict(zip(names, refs))
    x, counts, table_hbm = refs["x"], refs["counts"], refs["table"]
    one_ref, two_ref, eff, band, sems = (refs[name] for name in ("one", "two", "eff", "band", "sems"))
    chans = eff.shape[0]
    total, length = x.shape
    segs, half = total // chans, chans // 2
    even = lax.axis_index("chan") & 1 == 0
    buffers, had = refs.get("buffers"), first + (refs["table_in"].shape[0] if "table_in" in refs else 0)

    def fetch(tile):
        source = table_hbm.at[lax.axis_index("freq"), tile]
        target = refs["table_out"].at[tile - stop] if tile >= stop else buffers.at[tile - had]
        return pltpu.make_async_copy(source, target, sems.at[tile - first])

    def table_of(tile):
        return refs["table_in"].at[tile - first] if tile < had else buffers.at[tile - had]

    def spectrum_of(tile):
        if tile < first:
            return refs["spectrum_in"]
        return refs["spectrum_out"] if tile == stop - 1 <= tiles - 1 else refs["spectra"].at[tile - first]

    def power_of(tile):
        if tile < first:
            return refs["power_in"].at[tile - first + 2]
        return refs["power_out"].at[tile - stop + 2] if stop - 2 <= tile and stop <= tiles else refs["power"].at[tile - first]

    def store(tile, rows):
        block = jnp.dot(x[rows], table_of(tile)[...], preferred_element_type=jnp.float32)
        spectrum_of(tile)[rows] = block
        re, im = block[:, :TILE], block[:, TILE:]
        power_of(tile)[rows] = (re * re + im * im).astype(jnp.bfloat16)

    def finish(tile):
        window = jnp.dot(power_of(tile)[...], band[TILE : 2 * TILE], preferred_element_type=jnp.float32)
        window += jnp.dot(power_of(tile + 1)[...], band[2 * TILE :], preferred_element_type=jnp.float32)
        if tile:
            window += jnp.dot(power_of(tile - 1)[...], band[:TILE], preferred_element_type=jnp.float32)
        bin_index = tile * TILE + lax.broadcasted_iota(jnp.int32, (1, TILE), 1)
        number = jnp.minimum(bin_index + HALF, F - 1) - jnp.maximum(bin_index - HALF, 0) + 1
        inverse = 1.0 / number.astype(jnp.float32)
        at = (tile - max(first - 1, 0)) * 2 * TILE
        for seg in range(segs):
            rows = slice(seg * chans, (seg + 1) * chans)
            scale = lax.rsqrt(window[rows] * inverse + EPSILON)
            scale = jnp.where(eff[...] > seg, scale, 0.0)
            place = slice(seg * half, (seg + 1) * half)
            for lane in (0, TILE):
                white = spectrum_of(tile)[rows, lane : lane + TILE] * scale
                lo, hi = white[:half], white[half:]
                one_ref[place, at + lane : at + lane + TILE] = jnp.where(even, hi, lo).astype(jnp.bfloat16)
                two_ref[place, at + lane : at + lane + TILE] = jnp.where(even, lo, hi).astype(jnp.bfloat16)

    rows = slice(0, total)
    if first:
        head = max(had, first + 1)
        own = [fetch(tile) for tile in range(had, head)]
        stretches = [(own, [(tile, rows) for tile in range(first, head)])]
    else:
        head = 2
        vectors, load_sems = refs["vectors"], refs["load_sems"]
        early = (segs + 1) // 2
        loads = []
        for seg in range(segs):
            place = pl.ds(seg * chans, chans)
            loads.append(pltpu.make_async_copy(refs["x_hbm"].at[place], x.at[place], load_sems.at[seg]))
        whole = [
            pltpu.make_async_copy(refs["counts_hbm"], vectors.at[0], load_sems.at[segs]),
            pltpu.make_async_copy(refs["alive_hbm"], vectors.at[1], load_sems.at[segs + 1]),
        ]
        stretches = [
            ([fetch(0), *loads[:early], *whole], [(0, slice(0, early * chans))]),
            ([*loads[early:], fetch(1)], [(0, slice(early * chans, total)), (1, rows)]),
        ]
    if (stop - head) % 2:
        stretches.append(([fetch(head)], [(head, rows)]))
        head += 1
    for tile in range(head, stop, 2):
        stretches.append(([fetch(tile), fetch(tile + 1)], [(tile, rows), (tile + 1, rows)]))
    stretches.append(([fetch(tile) for tile in range(stop, further)], []))
    for copy in stretches[0][0]:
        copy.start()
    row = lax.broadcasted_iota(jnp.int32, (3 * TILE, TILE), 0)
    column = lax.broadcasted_iota(jnp.int32, (3 * TILE, TILE), 1)
    band[...] = (jnp.abs(row - TILE - column) <= HALF).astype(jnp.float32).astype(jnp.bfloat16)

    def limits():
        left = counts[0:1, :] - (lax.axis_index("seg") * segs).astype(jnp.float32)
        eff[...] = jnp.transpose(jnp.broadcast_to(left, (chans, chans)))

    if first:
        limits()
    for index, (copies, products) in enumerate(stretches[:-1]):
        for copy in stretches[index + 1][0]:
            copy.start()
        for copy in copies:
            copy.wait()
        if not first and index == 0:
            counts[0:1] = jnp.where(vectors[1] > 0, vectors[0], 0).astype(jnp.float32)
            counts[1:2] = vectors[0].astype(jnp.float32)
            limits()
            row = jnp.broadcast_to(counts[1:2, :].astype(jnp.bfloat16), (EXTRA, chans))
            for ref in (one_ref, two_ref):
                for lane in range(0, ref.shape[1], chans):
                    ref[segs * half :, lane : lane + chans] = row
        for product in products:
            store(*product)
    for tile in range(max(first - 1, 0), stop - 1):
        finish(tile)
    for copy in stretches[-1][0]:
        copy.wait()


def held(arrays):
    return [pltpu.with_memory_space_constraint(array, pltpu.VMEM) for array in arrays]


def whiten(plan, given, table, segs, chans):
    first, stop, further, tiles = plan
    total, length = segs * chans, table.shape[2]
    made = stop - first
    done = stop - 1 - max(first - 1, 0)
    send = total // 2 + (0 if first else EXTRA)
    here, away = pl.BlockSpec(memory_space=pltpu.VMEM), pl.BlockSpec(memory_space=pl.ANY)
    outs = {name: pltpu.VMEM((send, 2 * TILE * done), jnp.bfloat16) for name in ("one", "two")}
    handed = {}
    scratch = {
        "spectra": pltpu.VMEM((made, total, 2 * TILE), jnp.float32),
        "power": pltpu.VMEM((made, total, TILE), jnp.bfloat16),
        "band": pltpu.VMEM((3 * TILE, TILE), jnp.bfloat16),
        "eff": pltpu.VMEM((chans, chans), jnp.float32),
        "sems": pltpu.SemaphoreType.DMA((max(further, stop) - first,)),
    }
    lacking = made - (given["table_in"].shape[0] if "table_in" in given else 0)
    if lacking:
        scratch["buffers"] = pltpu.VMEM((lacking, length, 2 * TILE), jnp.bfloat16)
    if not first:
        handed["x"] = pltpu.VMEM((total, length), jnp.bfloat16)
        handed["counts"] = pltpu.VMEM((2, chans), jnp.float32)
        scratch["vectors"] = pltpu.VMEM((2, 1, chans), jnp.int32)
        scratch["load_sems"] = pltpu.SemaphoreType.DMA((segs + 2,))
    if stop <= tiles:
        handed["spectrum_out"] = pltpu.VMEM((total, 2 * TILE), jnp.float32)
        handed["power_out"] = pltpu.VMEM((2, total, TILE), jnp.bfloat16)
    if further > stop:
        handed["table_out"] = pltpu.VMEM((further - stop, length, 2 * TILE), jnp.bfloat16)
    if first:
        operands = held(given.values())
    else:
        operands = [pltpu.with_memory_space_constraint(array, pltpu.HBM) for array in given.values()]
    names = ["table", *given, *outs, *handed, *scratch]
    results = pl.pallas_call(
        functools.partial(whiten_kernel, plan, names),
        out_shape=[*outs.values(), *handed.values()],
        in_specs=[away] + [here if first else away] * len(operands),
        out_specs=[here] * (len(outs) + len(handed)),
        scratch_shapes=list(scratch.values()),
        compiler_params=pltpu.CompilerParams(vmem_limit_bytes=24 * MIB),
        cost_estimate=pl.CostEstimate(
            flops=2 * total * length * 2 * TILE * made,
            bytes_accessed=2 * length * 2 * TILE * made + 2 * total * length,
            transcendentals=0,
        ),
        name="whiten",
    )(table, *operands)
    handed = dict(zip(handed, results[2:]))
    kept = {name: handed.get(name, given.get(name)) for name in ("x", "counts")}
    passed = {name.replace("_out", "_in"): array for name, array in handed.items() if name.endswith("_out")}
    return results[0], results[1], {**kept, **passed}


def window_start(offset, chans):
    return jnp.minimum(chans // 2, chans - offset) // 16 * 16


def correlate_kernel(plan, offsets, one_ref, two_ref, got_one_ref, got_two_ref, table_hbm, *refs):
    tile_first, is_first, is_last = plan
    refs = list(refs)
    earlier = refs.pop(0)
    if is_last:
        keep_ref, send_ref = refs.pop(0), refs.pop(0)
    else:
        total = refs.pop(0)
    if is_first:
        inverse_ref = refs.pop(0)
    if is_last:
        total = refs.pop(0)
    select, frame, far, cross, delay, sems = refs
    tiles, segs, span, _ = frame.shape
    chans, half = span // 2, span // 4
    slots = cross.shape[0] // chans
    parts, depth, width = delay.shape
    last_place, length = table_hbm.shape[1] - 1, table_hbm.shape[2] // parts
    place = lax.axis_index("chan")
    even = place & 1 == 0
    known = jnp.where(place < lax.axis_size("chan") - 1, 4 * half, 3 * half)

    copies = []
    for part in range(parts):
        rows = pl.ds(part * length + tile_first * 2 * TILE, depth)
        source = table_hbm.at[lax.axis_index("freq"), last_place, rows, :]
        copies.append(pltpu.make_async_copy(source, delay.at[part], sems.at[part]))
        copies[part].start()

    row = lax.broadcasted_iota(jnp.int32, (chans, 2 * chans), 0)
    column = lax.broadcasted_iota(jnp.int32, (chans, 2 * chans), 1)
    for slot in range(slots):
        offset = offsets[slot]
        match = (column == row + window_start(offset, chans) + offset) & (column < known)
        select[slot * chans : (slot + 1) * chans] = match.astype(jnp.float32).astype(jnp.bfloat16)
    if is_first:
        row = lax.broadcasted_iota(jnp.int32, (chans, chans), 0)
        column = lax.broadcasted_iota(jnp.int32, (chans, chans), 1)
        own = earlier[1:2, :]
        following = [ref[segs * half :, :chans].astype(jnp.float32)[:1] for ref in (got_one_ref, got_two_ref)]
        following = jnp.where(even, *following)
        mine = jnp.sum(jnp.where(row == column, own, 0.0), axis=1, keepdims=True)
        for slot in range(slots):
            target = row + offsets[slot]
            partner = jnp.where(column == target, own, 0.0) + jnp.where(column + chans == target, following, 0.0)
            partner = jnp.sum(partner, axis=1, keepdims=True)
            divisor = jnp.maximum(jnp.minimum(mine, partner), 1.0)
            inverse_ref[slot] = jnp.broadcast_to(1.0 / divisor, inverse_ref.shape[1:])
    if is_last:
        keep_ref[...] = jnp.zeros_like(keep_ref)
        send_ref[...] = jnp.zeros_like(send_ref)

    order = ((one_ref, 2, 1), (two_ref, 1, 2), (got_one_ref, 3, 0), (got_two_ref, 0, 3))
    done = 0
    for tile in range(tiles):
        for ref, if_even, if_odd in order:
            spot = pl.ds(pl.multiple_of(jnp.where(even, if_even * half, if_odd * half), half), half)
            for seg in range(segs):
                rows = slice(seg * half, (seg + 1) * half)
                frame[tile, seg, spot, :] = ref[rows, tile * 2 * TILE : (tile + 1) * 2 * TILE]
        turn = tile % far.shape[0]
        for seg in range(segs):
            far[turn, seg] = jnp.dot(select[...], frame[tile, seg], preferred_element_type=jnp.float32)
        for slot in range(slots):
            start = window_start(offsets[slot], chans)
            for index in range(chans // 16):
                real = jnp.zeros((16, TILE), jnp.float32)
                imag = jnp.zeros((16, TILE), jnp.float32)
                base = pl.multiple_of(start + index * 16, 16)
                spot = slice(slot * chans + index * 16, slot * chans + index * 16 + 16)
                for seg in range(segs):
                    own = frame[tile, seg, pl.ds(base, 16), :].astype(jnp.float32)
                    own_re, own_im = own[:, :TILE], own[:, TILE:]
                    far_re, far_im = far[turn, seg, spot, :TILE], far[turn, seg, spot, TILE:]
                    real += own_re * far_re + own_im * far_im
                    imag += own_im * far_re - own_re * far_im
                lane = tile * 2 * TILE
                cross[spot, lane : lane + TILE] = real.astype(jnp.bfloat16)
                cross[spot, lane + TILE : lane + 2 * TILE] = imag.astype(jnp.bfloat16)
        if tile + 1 < tiles and (tile + 1) % LAG_TILES:
            continue
        lanes = slice(done * 2 * TILE, (tile + 1) * 2 * TILE)
        for part in range(parts):
            if not done:
                copies[part].wait()
            for slot in range(slots):
                spot, columns = slice(slot * chans, (slot + 1) * chans), slice(part * width, (part + 1) * width)
                term = jnp.dot(cross[spot, lanes], delay[part, lanes], preferred_element_type=jnp.float32)
                if done:
                    term += total[spot, columns]
                elif not is_first:
                    term += earlier[spot, columns]
                if not is_last or tile + 1 < tiles:
                    total[spot, columns] = term
                    continue
                rows = pl.ds(pl.multiple_of(window_start(offsets[slot], chans), 16), chans)
                if part == 0:
                    keep_ref[slot, rows, :] = term
                else:
                    send_ref[slot, rows, (part - 1) * width : part * width] = term.astype(send_ref.dtype)
        done = tile + 1


def correlate(plan, offsets, sent, got, table, earlier, segs, chans):
    tile_first, is_first, is_last = plan
    half, columns = chans // 2, sent[0].shape[1]
    tiles = columns // (2 * TILE)
    slots = offsets.shape[0]
    parts, keep = table.shape[0], table.shape[3]
    lags = parts * keep
    here = pl.BlockSpec(memory_space=pltpu.VMEM)
    scratch = [
        pltpu.VMEM((slots * chans, 2 * chans), jnp.bfloat16),
        pltpu.VMEM((tiles, segs, 2 * chans, 2 * TILE), jnp.bfloat16),
        pltpu.VMEM((2, segs, slots * chans, 2 * TILE), jnp.float32),
        pltpu.VMEM((slots * chans, columns), jnp.bfloat16),
        pltpu.VMEM((parts, columns, keep), jnp.bfloat16),
        pltpu.SemaphoreType.DMA((parts,)),
    ]
    if is_last:
        out_shape = [
            pltpu.VMEM((slots, 3 * half, keep), jnp.float32),
            pltpu.VMEM((slots, 3 * half, lags - keep), jnp.bfloat16),
        ]
        scratch = [pltpu.VMEM((slots * chans, lags), jnp.float32)] + scratch
    else:
        out_shape = [pltpu.VMEM((slots * chans, lags), jnp.float32)]
    if is_first:
        out_shape += [pltpu.VMEM((slots, chans, keep), jnp.float32)]
    return pl.pallas_call(
        functools.partial(correlate_kernel, plan),
        out_shape=out_shape,
        grid_spec=pltpu.PrefetchScalarGridSpec(
            num_scalar_prefetch=1,
            grid=(),
            in_specs=[here] * 4 + [pl.BlockSpec(memory_space=pl.ANY), here],
            out_specs=[here] * len(out_shape),
            scratch_shapes=scratch,
        ),
        compiler_params=pltpu.CompilerParams(vmem_limit_bytes=20 * MIB),
        cost_estimate=pl.CostEstimate(
            flops=tiles * 2 * slots * chans * 2 * TILE * (segs * 2 * chans + lags),
            bytes_accessed=tiles * (4 * segs * half * 2 * TILE * 2),
            transcendentals=0,
        ),
        name="correlate",
    )(offsets, *held([*sent, *got]), table, *held([earlier]))


def swap(block, first):
    blocks, parts = lax.axis_size("chan"), lax.axis_size("freq")
    route = []
    for i in range(blocks):
        partner = i + 1 if (i - first) % 2 == 0 else i - 1
        alone = not 0 <= partner < blocks
        for part in range(parts):
            target = i * parts + (part + 1) % parts if alone else partner * parts + part
            route.append((i * parts + part, target))
    return lax.ppermute(block, ("chan", "freq"), route)


def returns(blocks, parts):
    near, far = {}, {}
    last = blocks - 1
    for i in range(blocks):
        near[i, 1] = (i - 1, 1) if i else (0, 0)
        near[i, 0] = (i + 1, 0) if i < last else (last, 1)
        far[i, 0] = (i - 1, 1) if i else (0, 0)
        far[i, 1] = (i + 1, 0) if i < last else (last, 1)
    routes = []
    for steps in (near, far):
        route = []
        for source, target in steps.items():
            for part in range(parts):
                end = (part + 1) % parts if source == target else part
                route.append(((2 * source[0] + source[1]) * parts + part, (2 * target[0] + target[1]) * parts + end))
        routes.append(route)
    return routes


def reduced(span, keep, chans, has_next):
    spans, blocks = lax.axis_size("seg"), lax.axis_size("chan")
    half = chans // 2
    back = lax.ppermute(keep[:, :half].astype(jnp.bfloat16), "chan", [(i, (i - 1) % blocks) for i in range(blocks)])
    back = jnp.where(has_next, back.astype(jnp.float32), 0.0)
    keep = keep[:, half:] + jnp.pad(back, ((0, 0), (chans - half, 0), (0, 0)))
    piece = chans // spans
    result = lax.dynamic_slice_in_dim(keep, span * piece, piece, 1)
    for step in range(1, spans):
        target = lax.rem(span + step, spans)
        block = lax.dynamic_slice_in_dim(keep, target * piece, piece, 1).astype(jnp.bfloat16)
        block = lax.ppermute(block, "seg", [(i, (i + step) % spans) for i in range(spans)])
        result = result + block.astype(jnp.float32)
    return result


def shards(traces, dead_mask, seg_counts, offsets):
    segs, chans, length = traces.shape
    half = chans // 2
    parts, spans, blocks = lax.axis_size("freq"), lax.axis_size("seg"), lax.axis_size("chan")
    assert parts == 2
    table = jnp.asarray(tables(length, parts))
    tiles = table.shape[1] - 2
    span = lax.axis_index("seg").astype(jnp.int32)
    has_next = lax.axis_index("chan") < blocks - 1
    given = {
        "x_hbm": traces.reshape(segs * chans, length),
        "counts_hbm": seg_counts.reshape(1, chans),
        "alive_hbm": dead_mask.reshape(1, chans),
    }
    groups, made = [], 0
    for stop, further in zip(GROUPS, AHEAD):
        one, two, given = whiten((made, stop, further, tiles), given, table, segs, chans)
        groups.append((max(made - 1, 0), segs, (one, two), (swap(one, 0), swap(two, 1))))
        made = stop
    earlier = given["counts"]
    for index, (tile_first, number, sent, got) in enumerate(groups):
        plan = (tile_first, index == 0, index == len(groups) - 1)
        results = list(correlate(plan, offsets, sent, got, table, earlier, number, chans))
        if index == 0:
            inverse = results.pop()
        earlier = results[0]
    keep, send = results
    keep = keep + lax.ppermute(send, "freq", [(0, 1), (1, 0)]).astype(jnp.float32)
    if spans == 2:
        lower, upper = keep[:, half:chans], keep[:, chans:]
        mine = jnp.where(span == 0, lower, upper)
        other = jnp.where(span == 0, upper, lower).astype(jnp.bfloat16)
        back = keep[:, :half].astype(jnp.bfloat16)
        other = lax.ppermute(other, "seg", [(0, 1), (1, 0)])
        route_near, route_far = returns(blocks, parts)
        near = lax.ppermute(back, ("chan", "seg", "freq"), route_near)
        far = lax.ppermute(back, ("chan", "seg", "freq"), route_far)
        returned = jnp.where(has_next & (span == 1), near.astype(jnp.float32) + far.astype(jnp.float32), 0.0)
        result = mine + other.astype(jnp.float32) + returned
        result = result * jnp.where(span == 0, inverse[:, :half], inverse[:, half:])
    else:
        piece = chans // spans
        result = reduced(span, keep, chans, has_next)
        result = result * lax.dynamic_slice_in_dim(inverse, span * piece, piece, 1)
    return jnp.transpose(result, (1, 0, 2))


def solution(mesh):
    in_specs = (
        P("seg", ("groups", "chan"), None),
        P(("groups", "chan")),
        P(("groups", "chan")),
        P(),
    )
    out_specs = P(("groups", "chan", "seg"), None, "freq")
    return jax.shard_map(shards, mesh=mesh, in_specs=in_specs, out_specs=out_specs, check_vma=False)
```
